512 devices in a mesh: lat: 16 (over z_lo, core), lon: 32 (over z_hi, x, y).
Axes of the slice: x: 4, y: 4, z: 16 (z_hi: 2, z_lo: 8; z = z_hi * 8 + z_lo), core: 2. Of those that a mesh axis runs over, the one named last changes fastest.
Arguments:
- tokens: bfloat16 [1, 192, 384, 512], P(None, 'lat', 'lon'), may hold values from -8 to 8
- gain_first: float32 [512], replicated, may hold values from 0.1 to 1.9
- qkv_first: bfloat16 [512, 1536], replicated, may hold values from -16 to 16
- proj_first: bfloat16 [512, 512], replicated, may hold values from -0.25 to 0.25
- bias_first: float32 [16, 16, 529], P('lat'), may hold values from -6 to 6
- gain_second: float32 [512], replicated, may hold values from 0.1 to 1.9
- qkv_second: bfloat16 [512, 1536], replicated, may hold values from -16 to 16
- proj_second: bfloat16 [512, 512], replicated, may hold values from -0.25 to 0.25
- bias_second: float32 [16, 16, 529], P('lat'), may hold values from -6 to 6
Outputs:
- mixed: bfloat16 [1, 192, 384, 512], P(None, 'lat', 'lon')
The draws below stay inside these ranges and needn't reach their ends.
All inputs are finite; a program needn't handle non-finite values.
Results may differ from the reference program's by a relative error of at most 0.012.
The reference program's roundings to bfloat16 on the way count: a program that leaves them out, or rounds other values in their place, can miss the bound.
Values may be sent and summed in bfloat16 or wider, within the bound.
A program may use at most 64 MiB of HBM per device.

```python
import jax
import jax.numpy as jnp
from jax import lax

D = 512
HEADS = 16
LEV = 1
WH = 12
WW = 12
NREL = 529
NLW = 16
NY = 192
NX = 384


def draw_tokens(key, part):
    own = jax.random.fold_in(key, 3)
    base = jnp.clip(jax.random.normal(own, (LEV, NY, NX, D), jnp.float32), -6.0, 6.0)
    return base.astype(jnp.bfloat16)


def projection_law(key):
    scale = D ** (-0.5)
    w_query = jnp.clip(jax.random.normal(jax.random.fold_in(key, 1), (D, D), jnp.float32), -5.0, 5.0) * scale
    w_value = jnp.clip(jax.random.normal(jax.random.fold_in(key, 2), (D, D), jnp.float32), -5.0, 5.0) * scale
    w_keys = jnp.clip(jax.random.normal(jax.random.fold_in(key, 3), (D, D), jnp.float32), -5.0, 5.0) * scale
    joined = jnp.concatenate([w_query, w_keys, w_value], axis=1)
    return jnp.clip(joined, -16.0, 16.0).astype(jnp.bfloat16)


def draw_qkv_first(key, part):
    return projection_law(jax.random.fold_in(key, 11))


def draw_qkv_second(key, part):
    return projection_law(jax.random.fold_in(key, 12))


def block_scale(own_key, shape, pieces, low, top_value):
    level, own = 1.0, jax.random.fold_in(own_key, 6)
    for axis_at, shards_of in pieces:
        draws = jnp.exp(jax.random.uniform(jax.random.fold_in(own, axis_at), (shards_of,), jnp.float32, low / len(pieces), top_value / len(pieces)))
        level = level * jnp.repeat(draws, shape[axis_at] // shards_of).reshape([-1 if axis == axis_at else 1 for axis in range(len(shape))])
    return level


def scatter_about(key, shape, deviation, bound, pieces=(), held_as=jnp.bfloat16):
    entries = deviation * jax.random.normal(key, shape, jnp.float32)
    if pieces:
        entries = entries * block_scale(key, shape, pieces, -0.22, 0.18)
    return jnp.clip(entries, -bound, bound).astype(held_as)


def setup_inputs(seed: int = 0) -> dict:
    arg_keys = jax.random.split(jax.random.key(seed), 10)
    return {
        "tokens": draw_tokens(jax.random.fold_in(arg_keys[9], 71), 0),
        "gain_first": jnp.clip(1.0 + 0.18 * jax.random.normal(arg_keys[1], (D,), jnp.float32), 0.1, 1.9),
        "qkv_first": draw_qkv_first(jax.random.fold_in(arg_keys[9], 71), 0),
        "proj_first": scatter_about(arg_keys[3], (D, D), D ** -0.5, 0.25),
        "bias_first": scatter_about(arg_keys[4], (NLW, HEADS, NREL), 1.0, 6.0, ((0, 16),), jnp.float32),
        "gain_second": jnp.clip(1.0 + 0.18 * jax.random.normal(arg_keys[5], (D,), jnp.float32), 0.1, 1.9),
        "qkv_second": draw_qkv_second(jax.random.fold_in(arg_keys[9], 71), 0),
        "proj_second": scatter_about(arg_keys[7], (D, D), D ** -0.5, 0.25),
        "bias_second": scatter_about(arg_keys[8], (NLW, HEADS, NREL), 1.0, 6.0, ((0, 16),), jnp.float32),
    }


def offsets():
    count = LEV * WH * WW
    index = jnp.arange(count, dtype=jnp.int32)
    level = index // (WH * WW)
    row = index // WW % WH
    column = index % WW
    first = level[:, None] - level[None, :] + LEV - 1
    second = row[:, None] - row[None, :] + WH - 1
    third = column[:, None] - column[None, :] + WW - 1
    return ((first * (2 * WH - 1) + second) * (2 * WW - 1) + third).astype(jnp.int32)

def to_windows(tile):
    levels, rows, cols, width = tile.shape
    shaped = tile.reshape(levels, rows, cols // WW, WW, width)
    return shaped.transpose(2, 0, 1, 3, 4).reshape(cols // WW, levels * rows * WW, width)

def from_windows(wins, cols):
    width = wins.shape[-1]
    shaped = wins.reshape(cols // WW, LEV, WH, WW, width)
    return shaped.transpose(1, 2, 0, 3, 4).reshape(LEV, WH, cols, width)

def norm_rows(values, gain):
    data = values.astype(jnp.float32)
    mean = lax.optimization_barrier(jnp.mean(data, axis=-1, keepdims=True))
    centred = data - mean
    var = lax.optimization_barrier(jnp.mean(centred * centred, axis=-1, keepdims=True))
    return (centred * lax.rsqrt(var + 1e-05) * gain).astype(jnp.bfloat16)

def attend(normed, wqkv, wproj, bias, allowed):
    count = normed.shape[0]
    size = normed.shape[1]
    width = normed.shape[2]
    head_dim = width // HEADS
    mixed = jnp.dot(normed.reshape(-1, width), wqkv, preferred_element_type=jnp.float32)
    mixed = mixed.reshape(count, size, 3, HEADS, head_dim)
    query = mixed[:, :, 0]
    keys = mixed[:, :, 1]
    values = mixed[:, :, 2].astype(jnp.bfloat16)
    scores = jnp.einsum('wqhd,wkhd->whqk', query, keys, precision=lax.Precision.HIGHEST)
    scores = scores * head_dim ** (-0.5) + bias[None]
    scores = jnp.where(allowed[None, None], scores, -1e+30)
    top = lax.optimization_barrier(jnp.max(scores, axis=-1, keepdims=True))
    expo = jnp.exp(scores - top)
    weights = (expo / lax.optimization_barrier(jnp.sum(expo, axis=-1, keepdims=True))).astype(jnp.bfloat16)
    heads_out = jnp.einsum('whqk,wkhd->wqhd', weights.astype(jnp.float32), values.astype(jnp.float32))
    heads_out = heads_out.reshape(count * size, width).astype(jnp.bfloat16)
    return jnp.dot(heads_out, wproj, preferred_element_type=jnp.float32).reshape(count, size, width)

def section(inputs, gain, wqkv, wproj, table, shifted):
    rel = offsets()
    count = LEV * WH * WW
    index = jnp.arange(count, dtype=jnp.int32)
    lower = index // WW % WH >= WH // 2
    total_rows = inputs.shape[1]
    total_cols = inputs.shape[2]
    nrows = total_rows // WH
    if shifted:
        inputs = jnp.roll(inputs, (-(WH // 2), -(WW // 2)), axis=(1, 2))

    def one_row(i):
        rows = lax.dynamic_slice_in_dim(inputs, i * WH, WH, 1)
        wins = to_windows(rows)
        normed = norm_rows(wins, gain)
        bias = jnp.take(lax.dynamic_index_in_dim(table, i, 0, keepdims=False), rel, axis=1)
        if shifted:
            group = jnp.logical_and(lower, i == nrows - 1)
        else:
            group = jnp.zeros((count,), dtype=bool)
        allowed = group[:, None] == group[None, :]
        result = wins.astype(jnp.float32) + attend(normed, wqkv, wproj, bias, allowed)
        return from_windows(result.astype(jnp.bfloat16), total_cols)
    blocks = lax.map(one_row, jnp.arange(nrows, dtype=jnp.int32))
    result = blocks.transpose(1, 0, 2, 3, 4).reshape(LEV, total_rows, total_cols, inputs.shape[3])
    if shifted:
        result = jnp.roll(result, (WH // 2, WW // 2), axis=(1, 2))
    return result

def reference(tokens, gain_first, qkv_first, proj_first, bias_first, gain_second, qkv_second, proj_second, bias_second):
    first = section(tokens, gain_first, qkv_first, proj_first, bias_first, False)
    return section(first, gain_second, qkv_second, proj_second, bias_second, True)
```

```python
import functools
import math

import jax
import jax.numpy as jnp
import numpy as np
from jax import lax
from jax.experimental import pallas as pl
from jax.experimental.pallas import tpu as pltpu
from jax.sharding import PartitionSpec as P

HEADS = 16
WIN = 12
HALF = 6
TOK = 144
DIM = 512
LOG2E = math.log2(math.e)
MESH = pl.DeviceIdType.MESH
F32 = jnp.float32
BF16 = jnp.bfloat16


def own_at(r, c):
    return (c // HALF) * 72 + (r // HALF) * 36 + (r % HALF) * HALF + c % HALF


def constants():
    out = {}
    p0 = np.zeros((288, 192), np.float32)
    back = np.zeros((192, TOK), np.float32)
    for r in range(WIN):
        for c in range(WIN):
            p0[own_at(r, c), r * 16 + c] = 1
            p0[TOK + 143 - (r * WIN + c), r * 16 + c] = 1
            back[r * 16 + c, own_at(r, c)] = 1
    rep = np.zeros((576, TOK), np.float32)
    fold = np.zeros((TOK, 576), np.float32)
    for r in range(WIN):
        for h in range(4):
            for c in range(WIN):
                row = r * 48 + h * WIN + c
                rep[row, 143 - (r * WIN + c)] = 1
                fold[own_at(r, c), row] = 1
    rep2 = np.zeros((2, 288, TOK), np.float32)
    fold2 = np.zeros((2, 192, 288), np.float32)
    strip = np.zeros((2, 288, 416), np.float32)
    for b in range(2):
        for a in range(2):
            for r in range(HALF):
                for h in range(4):
                    for c in range(HALF):
                        row = a * TOK + r * 24 + h * HALF + c
                        rep2[b, row, b * 72 + a * 36 + r * HALF + c] = 1
                        fold2[b, (a * HALF + r) * 16 + b * HALF + c, row] = 1
            for r in range(WIN):
                for c in range(WIN):
                    at = (r % HALF) * HALF + c % HALF
                    own_row = (r >= HALF) == (a == 0)
                    own_col = (c >= HALF) == (b == 0)
                    if own_row and own_col:
                        src = b * 72 + a * 36 + at
                    elif own_col:
                        src = 144 + 48 * a + 8 * b + (4 if a == 0 else 0) + at
                    elif own_row:
                        src = 240 + 8 * (1 - b) + a * 36 + at
                    else:
                        src = 320 + 48 * a + 8 * (1 - b) + (4 if a == 0 else 0) + at
                    strip[b, a * TOK + 143 - (r * WIN + c), src] = 1
    pick = np.zeros((640, 384), np.float32)
    for u in range(23):
        for v in range(WIN):
            pick[u * 23 + v, u * WIN + v] = 1
    order1 = np.zeros((192, 192), np.float32)
    order2 = np.zeros((192, 192), np.float32)
    for h in range(HEADS):
        for c in range(WIN):
            order1[h * WIN + c, c * HEADS + h] = 1
            b = 1 if c < HALF else 0
            order2[b * 96 + h * HALF + c % HALF, c * HEADS + h] = 1
    out["p0"] = p0
    out["pick"] = pick
    out["order1"] = np.concatenate([order1, order1], axis=1)
    out["rep"] = rep
    out["fold"] = fold
    out["back"] = back
    out["order2"] = np.concatenate([order2, order2], axis=1)
    out["rep2"] = rep2
    out["fold2"] = fold2
    out["strip"] = strip
    return out


CONSTS = constants()
CNAMES = list(CONSTS)


def dot(a, b):
    return jnp.dot(a, b, preferred_element_type=F32)


def dot_nt(a, b):
    return lax.dot_general(a, b, (((1,), (1,)), ((), ())), preferred_element_type=F32)


def norm(data, gain):
    mean = jnp.mean(data, axis=-1, keepdims=True)
    centred = data - mean
    var = jnp.mean(centred * centred, axis=-1, keepdims=True)
    return (centred * lax.rsqrt(var + 1e-05) * gain).astype(BF16)


def split(values):
    high = values.astype(BF16)
    return high, (values - high.astype(F32)).astype(BF16)


def head_mask(size, width):
    row = lax.broadcasted_iota(jnp.int32, (4 * size, width), 0)
    lane = lax.broadcasted_iota(jnp.int32, (4 * size, width), 1)
    head = (row >= size).astype(jnp.int32) + (row >= 2 * size).astype(jnp.int32) + (row >= 3 * size).astype(jnp.int32)
    return head == ((lane // 32) & 3)


def masked(values, size):
    rows, width = values.shape
    mask = head_mask(size, width)
    kept = jnp.where(mask[None], values.reshape(rows // (4 * size), 4 * size, width), 0.0)
    return kept.reshape(rows, width).astype(BF16)


def offsets_table(table, padded, pick, order):
    padded[...] = jnp.zeros_like(padded)
    padded[:, :529] = table
    flat = padded[...] * LOG2E
    rows = jnp.concatenate([flat] + [pltpu.roll(flat, 640 - c, 1) for c in range(1, WIN)], axis=0)
    high, low = split(rows)
    parts = jnp.concatenate([dot(high, pick).astype(BF16), dot(low, pick).astype(BF16)], axis=0)
    return dot(order, parts)


def attend(qhi, qlo, khi, klo, val, bias, size):
    parts = []
    ones = jnp.ones((val.shape[0], 128), BF16)
    for g in range(4):
        at = slice(128 * g, 128 * g + 128)
        left = jnp.concatenate([qhi[:, at], qlo[:, at], qhi[:, at]], axis=1)
        right = jnp.concatenate([khi[:, at], khi[:, at], klo[:, at]], axis=1)
        scores = dot_nt(left, right) + bias(g)
        top = jnp.max(scores, axis=-1, keepdims=True)
        expo = jnp.exp2(scores - top).astype(BF16)
        both = dot(expo, jnp.concatenate([val[:, at], ones], axis=1))
        parts.append(masked(both[:, :128] / both[:, 128:], size))
    return jnp.concatenate(parts, axis=1)


def kernel(
    nlat, nlon, tok_h, gain1_h, wqkv1_h, wproj1_h, bias1_h, gain2_h, wqkv2_h, wproj2_h, bias2_h, *rest
):
    nc = len(CNAMES)
    const_h = dict(zip(CNAMES, rest[:nc]))
    out_h = rest[nc]
    (tok, gain1, wqkv1, wproj1, tab1, gain2, wqkv2, wproj2, tab2, tabn), rest = rest[nc + 1 : nc + 11], rest[nc + 11 :]
    const = dict(zip(CNAMES, rest[:nc]))
    (
        xpad, tpad, bias1, bias2, near, halo_lon, halo_lat, corner, result,
        in_sem, out_sem, lon_send, lon_recv, lat_send, lat_recv, cor_send, cor_recv, tab_send, tab_recv,
    ) = rest[nc:]

    lat = lax.axis_index("lat")
    lon = lax.axis_index("lon")
    north = lax.rem(lat + nlat - 1, nlat)
    south = lax.rem(lat + 1, nlat)
    west = lax.rem(lon + nlon - 1, nlon)
    east = lax.rem(lon + 1, nlon)
    has_n = lat > 0
    has_s = lat < nlat - 1

    barrier = pltpu.get_barrier_semaphore()
    for peer in ((lat, west), (lat, east), (north, lon), (south, lon)):
        pl.semaphore_signal(barrier, inc=1, device_id=peer, device_id_type=MESH)

    loads = {}
    order = [
        ("tok", tok_h, tok), ("p0", const_h["p0"], const["p0"]), ("tab1", bias1_h, tab1),
        ("pick", const_h["pick"], const["pick"]), ("gain1", gain1_h, gain1), ("order1", const_h["order1"], const["order1"]),
        ("wqkv1", wqkv1_h, wqkv1), ("rep", const_h["rep"], const["rep"]), ("fold", const_h["fold"], const["fold"]),
        ("wproj1", wproj1_h, wproj1), ("gain2", gain2_h, gain2), ("tab2", bias2_h, tab2),
        ("order2", const_h["order2"], const["order2"]), ("wqkv2", wqkv2_h, wqkv2), ("rep2", const_h["rep2"], const["rep2"]),
        ("strip", const_h["strip"], const["strip"]), ("back", const_h["back"], const["back"]),
        ("fold2", const_h["fold2"], const["fold2"]), ("wproj2", wproj2_h, wproj2),
    ]
    for i, (name, src, dst) in enumerate(order):
        loads[name] = pltpu.make_async_copy(src, dst, in_sem.at[i])
        loads[name].start()

    def get(name):
        loads[name].wait()

    get("tab1")
    get("pick")
    get("order1")
    table = offsets_table(tab1[0], tpad, const["pick"][...], const["order1"][...])
    for r in range(WIN):
        moved = table[:, WIN * r : WIN * r + TOK]
        for g in range(4):
            bias1[g, 48 * r : 48 * r + 48, :] = moved[48 * g : 48 * g + 48]

    get("tok")
    get("p0")
    xpad[...] = jnp.zeros_like(xpad)
    for r in range(WIN):
        xpad[16 * r : 16 * r + WIN, :] = tok[0, r]
    both = dot(const["p0"][...], xpad[...])
    mine = both[:TOK]
    get("gain1")
    normed = norm(both[TOK:], gain1[...])
    get("wqkv1")
    scale = LOG2E / math.sqrt(32.0)
    flat = dot(normed, wqkv1[...])
    qhi, qlo = split(flat[:, :DIM] * scale)
    khi, klo = split(flat[:, DIM : 2 * DIM])
    val = flat[:, 2 * DIM :].astype(BF16)
    get("rep")
    rep = const["rep"][...]
    heads = attend(
        masked(dot(rep, qhi), WIN), masked(dot(rep, qlo), WIN), khi, klo, val, lambda g: bias1[g], WIN
    )
    get("fold")
    get("wproj1")
    heads = dot(const["fold"][...], heads).astype(BF16)
    first = (mine + dot(heads, wproj1[...])).astype(BF16)
    get("gain2")
    normed = norm(first.astype(F32), gain2[...])
    own = result
    own[...] = normed

    get("tab2")
    pl.semaphore_wait(barrier, 4)

    def remote(src, dst, send, recv, peer):
        return pltpu.make_async_remote_copy(
            src_ref=src, dst_ref=dst, send_sem=send, recv_sem=recv, device_id=peer, device_id_type=MESH
        )

    to_w = remote(own.at[pl.ds(0, 80)], halo_lon.at[1], lon_send.at[0], lon_recv.at[1], (lat, west))
    to_e = remote(own.at[pl.ds(64, 80)], halo_lon.at[0], lon_send.at[1], lon_recv.at[0], (lat, east))
    to_w.start()
    to_e.start()
    to_n = [
        remote(own.at[pl.ds(64 * b, 48)], halo_lat.at[1, b], lat_send.at[0, b], lat_recv.at[1, b], (north, lon))
        for b in range(2)
    ]
    to_s = [
        remote(own.at[pl.ds(32 + 64 * b, 48)], halo_lat.at[0, b], lat_send.at[1, b], lat_recv.at[0, b], (south, lon))
        for b in range(2)
    ]

    @pl.when(has_n)
    def _():
        for copy in to_n:
            copy.start()

    @pl.when(has_s)
    def _():
        for copy in to_s:
            copy.start()

    send_tab = remote(tab2, tabn, tab_send, tab_recv, (south, lon))
    send_tab.start()

    @pl.when(lat == 0)
    def _():
        halo_lat[0] = jnp.zeros((2, 48, DIM), BF16)
        corner[0] = jnp.zeros((2, 48, DIM), BF16)

    @pl.when(lat == nlat - 1)
    def _():
        halo_lat[1] = jnp.zeros((2, 48, DIM), BF16)
        corner[1] = jnp.zeros((2, 48, DIM), BF16)

    get("order2")

    def window_bias(a, ref):
        table = offsets_table(ref[0], tpad, const["pick"][...], const["order2"][...])
        cut = jnp.logical_not(has_n if a == 0 else has_s)
        lane = lax.broadcasted_iota(jnp.int32, (1, TOK), 1)
        other = (lane >= 72) if a == 0 else (lane < 72)
        shut = jnp.where(other, jnp.where(cut, -1e30, 0.0), 0.0)
        for r in range(HALF):
            at = WIN * (r + (HALF if a == 0 else 0))
            moved = table[:, at : at + TOK] + shut
            for b in range(2):
                for g in range(4):
                    bias2[a, b, g, 24 * r : 24 * r + 24, :] = moved[96 * b + 24 * g : 96 * b + 24 * g + 24]

    window_bias(1, tab2)
    get("wqkv2")
    qhi, qlo = split(dot(normed, wqkv2[:, :DIM]) * scale)
    get("back")
    residual = dot(const["back"][...], first)
    get("rep2")
    get("strip")
    get("fold2")

    far_w = lax.rem(lon, nlon // 2) == 0
    side_far = jnp.where(far_w, 0, 1)
    side_near = 1 - side_far

    def relay(b):
        remote(own.at[pl.ds(0, 80)], halo_lon.at[b], lon_send.at[0], lon_recv.at[b], (lat, west)).wait_recv()

        @pl.when(has_n)
        def _():
            remote(halo_lon.at[b, pl.ds(0, 48)], corner.at[1, b], cor_send.at[0, b], cor_recv.at[1, b], (north, lon)).start()

        @pl.when(has_s)
        def _():
            remote(halo_lon.at[b, pl.ds(32, 48)], corner.at[0, b], cor_send.at[1, b], cor_recv.at[0, b], (south, lon)).start()

    def settle(b):
        for a, has in ((0, has_n), (1, has_s)):
            @pl.when(has)
            def _(a=a):
                remote(own.at[pl.ds(0, 48)], corner.at[a, b], cor_send.at[0, b], cor_recv.at[a, b], (north, lon)).wait_recv()

    def side(b):
        gathered = jnp.concatenate(
            [own[...], halo_lat[0, b], halo_lat[1, b], halo_lon[b], corner[0, b], corner[1, b]], axis=0
        )
        keys = dot(const["strip"][b], gathered).astype(BF16)
        flat = dot(keys, wqkv2[:, DIM:])
        khi, klo = split(flat[:, :DIM])
        val = flat[:, DIM:].astype(BF16)
        rep = const["rep2"][b]
        ahi = masked(dot(rep, qhi), HALF)
        alo = masked(dot(rep, qlo), HALF)
        parts = []
        for a in range(2):
            at = slice(TOK * a, TOK * a + TOK)
            parts.append(
                attend(ahi[at], alo[at], khi[at], klo[at], val[at], lambda g, a=a: bias2[a, b, g], HALF)
            )
        return dot(const["fold2"][b], jnp.concatenate(parts, axis=0))

    relay(side_near)
    remote(tab2, tabn, tab_send, tab_recv, (south, lon)).wait_recv()
    window_bias(0, tabn)
    for a, has in ((0, has_n), (1, has_s)):
        @pl.when(has)
        def _(a=a):
            for b in range(2):
                remote(own.at[pl.ds(0, 48)], halo_lat.at[a, b], lat_send.at[0, b], lat_recv.at[a, b], (north, lon)).wait_recv()

    settle(side_near)
    near[...] = side(side_near)
    relay(side_far)
    settle(side_far)
    heads = (near[...] + side(side_far)).astype(BF16)
    get("wproj2")
    mixed = (residual + dot(heads, wproj2[...])).astype(BF16)
    for r in range(WIN):
        tok[0, r] = mixed[16 * r : 16 * r + WIN]
    store = pltpu.make_async_copy(tok, out_h, out_sem)
    store.start()

    to_w.wait_send()
    to_e.wait_send()
    send_tab.wait_send()

    @pl.when(has_n)
    def _():
        for b in range(2):
            to_n[b].wait_send()
            remote(own.at[pl.ds(0, 48)], corner.at[1, b], cor_send.at[0, b], cor_recv.at[1, b], (north, lon)).wait_send()

    @pl.when(has_s)
    def _():
        for b in range(2):
            to_s[b].wait_send()
            remote(own.at[pl.ds(0, 48)], corner.at[0, b], cor_send.at[1, b], cor_recv.at[0, b], (south, lon)).wait_send()

    store.wait()


def shards(tokens, gain1, wqkv1, wproj1, bias1, gain2, wqkv2, wproj2, bias2):
    nlat = lax.axis_size("lat")
    nlon = lax.axis_size("lon")
    consts = [jnp.asarray(CONSTS[name], BF16) for name in CNAMES]
    dma = pltpu.SemaphoreType.DMA
    vmem = pltpu.VMEM
    args = [tokens, gain1.reshape(1, DIM), wqkv1, wproj1, bias1, gain2.reshape(1, DIM), wqkv2, wproj2, bias2]
    scratch = [vmem(x.shape, x.dtype) for x in args] + [vmem(bias2.shape, F32)]
    scratch += [vmem(x.shape, BF16) for x in consts]
    scratch += [
        vmem((192, DIM), BF16),
        vmem((HEADS, 640), F32),
        vmem((4, 576, TOK), F32),
        vmem((2, 2, 4, TOK, TOK), F32),
        vmem((192, DIM), F32),
        vmem((2, 80, DIM), BF16),
        vmem((2, 2, 48, DIM), BF16),
        vmem((2, 2, 48, DIM), BF16),
        vmem((TOK, DIM), BF16),
        dma((len(args) + len(consts),)),
        dma(()),
        dma((2,)), dma((2,)),
        dma((2, 2)), dma((2, 2)),
        dma((2, 2)), dma((2, 2)),
        dma(()), dma(()),
    ]
    anywhere = pl.BlockSpec(memory_space=pltpu.HBM)
    return pl.pallas_call(
        functools.partial(kernel, nlat, nlon),
        out_shape=jax.ShapeDtypeStruct(tokens.shape, BF16),
        in_specs=[anywhere] * (len(args) + len(consts)),
        out_specs=anywhere,
        scratch_shapes=scratch,
        compiler_params=pltpu.CompilerParams(
            collective_id=0, has_side_effects=True, vmem_limit_bytes=62 * 1024 * 1024
        ),
        cost_estimate=pl.CostEstimate(flops=2_000_000_000, bytes_accessed=8_000_000, transcendentals=700_000),
        name="pair",
    )(*args, *consts)


def solution(mesh):
    placed = (
        P(None, "lat", "lon", None), P(), P(), P(), P("lat", None, None), P(), P(), P(), P("lat", None, None),
    )
    return jax.shard_map(
        shards, mesh=mesh, in_specs=placed, out_specs=P(None, "lat", "lon", None), check_vma=False
    )
```

```python
import functools
import math

import jax
import jax.numpy as jnp
import numpy as np
from jax import lax
from jax.experimental import pallas as pl
from jax.experimental.pallas import tpu as pltpu
from jax.sharding import PartitionSpec as P

HEADS = 16
WIN = 12
HALF = 6
TOK = 144
DIM = 512
LOG2E = math.log2(math.e)
MESH = pl.DeviceIdType.MESH
F32 = jnp.float32
BF16 = jnp.bfloat16


def own_at(r, c):
    return (c // HALF) * 72 + (r // HALF) * 36 + (r % HALF) * HALF + c % HALF


def constants():
    p0 = np.zeros((288, 192), np.float32)
    back = np.zeros((192, TOK), np.float32)
    rep = np.zeros((576, TOK), np.float32)
    fold = np.zeros((TOK, 576), np.float32)
    for r in range(WIN):
        for c in range(WIN):
            flipped = 143 - (c * WIN + r)
            p0[own_at(r, c), r * 16 + c] = 1
            p0[TOK + flipped, r * 16 + c] = 1
            back[r * 16 + c, own_at(r, c)] = 1
            for h in range(4):
                rep[c * 48 + h * WIN + r, flipped] = 1
                fold[own_at(r, c), c * 48 + h * WIN + r] = 1
    rep2 = np.zeros((576, TOK), np.float32)
    fold2 = np.zeros((2, 192, 288), np.float32)
    early = np.zeros((288, 304), np.float32)
    late = np.zeros((TOK, 160), np.float32)
    for b in range(2):
        for a in range(2):
            for c in range(HALF):
                for r in range(HALF):
                    at = r * HALF + c
                    for h in range(4):
                        row = a * TOK + c * 24 + h * HALF + r
                        rep2[b * 288 + row, b * 72 + a * 36 + at] = 1
                        fold2[b, (a * HALF + r) * 16 + b * HALF + c, row] = 1
                    for whole in (r, r + HALF):
                        key = (HALF - 1 - c) * WIN + WIN - 1 - whole
                        mine = (whole >= HALF) == (a == 0)
                        src = b * 72 + a * 36 + at if mine else 144 + 40 * (2 * a + b) + at
                        early[b * 144 + a * 72 + key, src] = 1
                        late[a * 72 + key, 40 * a + at if mine else 80 + 40 * a + at] = 1
    pick = np.zeros((384, 384), np.float32)
    for v in range(23):
        for r in range(WIN):
            pick[r * 23 + v, v * WIN + r] = 1
    order1 = np.zeros((192, 192), np.float32)
    order2 = np.zeros((96, 96), np.float32)
    for h in range(HEADS):
        for r in range(WIN):
            order1[h * WIN + r, r * HEADS + h] = 1
        for r in range(HALF):
            order2[h * HALF + r, r * HEADS + h] = 1
    return {
        "p0": p0,
        "pick": pick,
        "order1": np.concatenate([order1, order1], axis=1),
        "rep": rep,
        "fold": fold,
        "back": back,
        "order2": np.concatenate([order2, order2], axis=1),
        "rep2": rep2,
        "early": early,
        "late": late,
        "fold2": fold2,
    }


CONSTS = constants()
CNAMES = list(CONSTS)


def dot(a, b):
    return jnp.dot(a, b, preferred_element_type=F32)


def dot_nt(a, b):
    return lax.dot_general(a, b, (((1,), (1,)), ((), ())), preferred_element_type=F32)


def norm(data, gain):
    mean = jnp.mean(data, axis=-1, keepdims=True)
    centred = data - mean
    var = jnp.mean(centred * centred, axis=-1, keepdims=True)
    return (centred * lax.rsqrt(var + 1e-05) * gain).astype(BF16)


def split(values):
    high = values.astype(BF16)
    return high, (values - high.astype(F32)).astype(BF16)


def head_mask(size, width):
    row = lax.broadcasted_iota(jnp.int32, (4 * size, width), 0)
    lane = lax.broadcasted_iota(jnp.int32, (4 * size, width), 1)
    head = (row >= size).astype(jnp.int32) + (row >= 2 * size).astype(jnp.int32) + (row >= 3 * size).astype(jnp.int32)
    return head == ((lane // 32) & 3)


def masked(values, size):
    rows, width = values.shape
    mask = head_mask(size, width)
    kept = jnp.where(mask[None], values.reshape(rows // (4 * size), 4 * size, width), 0.0)
    return kept.reshape(rows, width).astype(BF16)


def offsets_table(table, padded, pick, order, start, count):
    padded[...] = jnp.zeros_like(padded)
    padded[:, :529] = table
    flat = padded[...] * LOG2E
    moved = [pltpu.roll(flat, (640 - 23 * r) % 640, 1) if r else flat for r in range(start, start + count)]
    rows = jnp.concatenate([m[:, :384] for m in moved], axis=0)
    high, low = split(rows)
    parts = jnp.concatenate([dot(high, pick).astype(BF16), dot(low, pick).astype(BF16)], axis=0)
    return dot(order, parts)


def attend(qhi, qlo, khi, klo, val, bias, size):
    parts = []
    ones = jnp.ones((val.shape[0], 128), BF16)
    for g in range(4):
        at = slice(128 * g, 128 * g + 128)
        left = jnp.concatenate([qhi[:, at], qlo[:, at], qhi[:, at]], axis=1)
        right = jnp.concatenate([khi[:, at], khi[:, at], klo[:, at]], axis=1)
        scores = dot_nt(left, right) + bias(g)
        top = jnp.max(scores, axis=-1, keepdims=True)
        expo = jnp.exp2(scores - top).astype(BF16)
        both = dot(expo, jnp.concatenate([val[:, at], ones], axis=1))
        parts.append(masked(both[:, :128] / both[:, 128:], size))
    return jnp.concatenate(parts, axis=1)


def kernel(
    nlat, nlon, tok_h, gain1_h, wqkv1_h, wproj1_h, bias1_h, gain2_h, wqkv2_h, wproj2_h, bias2_h, *rest
):
    nc = len(CNAMES)
    const_h = dict(zip(CNAMES, rest[:nc]))
    out_h = rest[nc]
    (tok, gain1, wqkv1, wproj1, tab1, gain2, wqkv2, wproj2, tab2, tabn), rest = rest[nc + 1 : nc + 11], rest[nc + 11 :]
    const = dict(zip(CNAMES, rest[:nc]))
    (
        xpad, tpad, bias1, bias2, near, halo_lon, halo_lat, corner, own, pack, packed, unpack, keyval, ahi, alo,
        in_sem, out_sem, lon_send, lon_recv, lat_send, lat_recv, cor_send, cor_recv, tab_send, tab_recv,
    ) = rest[nc:]

    lat = lax.axis_index("lat")
    lon = lax.axis_index("lon")
    north = lax.rem(lat + nlat - 1, nlat)
    south = lax.rem(lat + 1, nlat)
    west = lax.rem(lon + nlon - 1, nlon)
    east = lax.rem(lon + 1, nlon)
    has_n = lat > 0
    has_s = lat < nlat - 1

    barrier = pltpu.get_barrier_semaphore()
    for peer in ((lat, west), (lat, east), (north, lon), (south, lon)):
        pl.semaphore_signal(barrier, inc=1, device_id=peer, device_id_type=MESH)

    loads = {}
    early_loads = [
        ("tab1", bias1_h, tab1), ("pick", const_h["pick"], const["pick"]), ("order1", const_h["order1"], const["order1"]),
        ("tok", tok_h, tok), ("p0", const_h["p0"], const["p0"]), ("gain1", gain1_h, gain1),
        ("wqkv1", wqkv1_h, wqkv1), ("rep", const_h["rep"], const["rep"]), ("fold", const_h["fold"], const["fold"]),
        ("wproj1", wproj1_h, wproj1), ("gain2", gain2_h, gain2), ("tab2", bias2_h, tab2),
    ]
    late_loads = [
        ("order2", const_h["order2"], const["order2"]), ("wqkv2", wqkv2_h, wqkv2), ("rep2", const_h["rep2"], const["rep2"]),
        ("back", const_h["back"], const["back"]), ("early", const_h["early"], const["early"]),
        ("late", const_h["late"], const["late"]), ("fold2", const_h["fold2"], const["fold2"]), ("wproj2", wproj2_h, wproj2),
    ]
    for i, (name, src, dst) in enumerate(early_loads + late_loads):
        loads[name] = pltpu.make_async_copy(src, dst, in_sem.at[i])
    for name, _, _ in early_loads:
        loads[name].start()

    def get(name):
        loads[name].wait()

    get("tab1")
    get("pick")
    get("order1")
    table = offsets_table(tab1[0], tpad, const["pick"][...], const["order1"][...], 0, WIN)
    for c in range(WIN):
        moved = table[:, WIN * c : WIN * c + TOK]
        for g in range(4):
            bias1[g, 48 * c : 48 * c + 48, :] = moved[48 * g : 48 * g + 48]

    get("tok")
    get("p0")
    xpad[...] = jnp.zeros_like(xpad)
    for r in range(WIN):
        xpad[16 * r : 16 * r + WIN, :] = tok[0, r]
    both = dot(const["p0"][...], xpad[...])
    mine = both[:TOK]
    get("gain1")
    normed = norm(both[TOK:], gain1[...])
    get("wqkv1")
    scale = LOG2E / math.sqrt(32.0)
    flat = dot(normed, wqkv1[...])
    qhi, qlo = split(flat[:, :DIM] * scale)
    khi, klo = split(flat[:, DIM : 2 * DIM])
    val = flat[:, 2 * DIM :].astype(BF16)
    get("rep")
    for name, _, _ in late_loads:
        loads[name].start()
    rep = const["rep"][...]
    heads = attend(
        masked(dot(rep, qhi), WIN), masked(dot(rep, qlo), WIN), khi, klo, val, lambda g: bias1[g], WIN
    )
    get("fold")
    get("wproj1")
    heads = dot(const["fold"][...], heads).astype(BF16)
    first = (mine + dot(heads, wproj1[...])).astype(BF16)
    get("gain2")
    normed = norm(first.astype(F32), gain2[...])
    own[...] = normed
    wide = normed.astype(F32)
    for a in range(2):
        for b in range(2):
            for j in range(4):
                at = 72 * b + 36 * a
                pack[a, b, 36 * j : 36 * j + 36, :] = wide[at : at + 36, 128 * j : 128 * j + 128]
    packed[...] = pack[...].astype(BF16)

    side_far = jnp.where(lax.rem(lon, nlon // 2) == 0, 0, 1)
    side_near = 1 - side_far
    border = jnp.logical_or(lax.rem(lon, nlon // 2) == 0, lax.rem(lon, nlon // 2) == nlon // 2 - 1)
    part0 = lax.rem(lat, 2)
    get("tab2")
    pl.semaphore_wait(barrier, 4)

    def remote(src, dst, send, recv, peer):
        return pltpu.make_async_remote_copy(
            src_ref=src, dst_ref=dst, send_sem=send, recv_sem=recv, device_id=peer, device_id_type=MESH
        )

    def edge(b, a):
        peer = jnp.where(b == 0, west, east)
        return remote(packed.at[a, b], halo_lon.at[1 - b, a], lon_send.at[b, a], lon_recv.at[1 - b, a], (lat, peer))

    for b in (side_far, side_near):
        for a in (part0, 1 - part0):
            edge(b, a).start()
    to_n = remote(packed.at[0], halo_lat.at[1], lat_send.at[0], lat_recv.at[1], (north, lon))
    to_s = remote(packed.at[1], halo_lat.at[0], lat_send.at[1], lat_recv.at[0], (south, lon))

    @pl.when(has_n)
    def _():
        to_n.start()

    @pl.when(has_s)
    def _():
        to_s.start()

    send_tab = remote(tab2, tabn, tab_send, tab_recv, (south, lon))
    send_tab.start()

    for a, has in ((0, has_n), (1, has_s)):
        @pl.when(jnp.logical_not(has))
        def _(a=a):
            halo_lat[a] = jnp.zeros((2, TOK, 128), BF16)
            for b in range(2):
                corner[b, a] = jnp.zeros((TOK, 128), BF16)

    get("order2")

    def window_bias(a, ref):
        start = HALF if a == 0 else 0
        table = offsets_table(ref[0], tpad, const["pick"][...], const["order2"][...], start, HALF)
        cut = jnp.logical_not(has_n if a == 0 else has_s)
        lane = lax.rem(lax.broadcasted_iota(jnp.int32, (1, TOK), 1), WIN)
        other = (lane >= HALF) if a == 0 else (lane < HALF)
        shut = jnp.where(other, jnp.where(cut, -1e30, 0.0), 0.0)
        for c in range(WIN):
            moved = table[:, WIN * c : WIN * c + TOK] + shut
            b = 0 if c >= HALF else 1
            row = 24 * (c % HALF)
            for g in range(4):
                bias2[a, b, g, row : row + 24, :] = moved[24 * g : 24 * g + 24]

    def relay(b):
        for a in (part0, 1 - part0):
            remote(packed.at[a, b], halo_lon.at[b, a], lon_send.at[b, a], lon_recv.at[b, a], (lat, west)).wait_recv()
            peer = jnp.where(a == 0, north, south)

            @pl.when(jnp.where(a == 0, lat > 0, lat < nlat - 1))
            def _(a=a, peer=peer):
                remote(
                    halo_lon.at[b, a], corner.at[b, 1 - a], cor_send.at[b, a], cor_recv.at[b, 1 - a], (peer, lon)
                ).start()

    def settle(b):
        for a, has in ((0, has_n), (1, has_s)):
            @pl.when(has)
            def _(a=a):
                remote(
                    halo_lon.at[b, a], corner.at[b, a], cor_send.at[b, a], cor_recv.at[b, a], (north, lon)
                ).wait_recv()

    def tokens_of(quadrants):
        for i, ref in enumerate(quadrants):
            data = ref[...].astype(F32)
            for j in range(4):
                unpack[40 * i : 40 * i + 36, 128 * j : 128 * j + 128] = data[36 * j : 36 * j + 36]
        return unpack[...].astype(BF16)

    def side(b):
        new = tokens_of([halo_lon.at[b, 0], halo_lon.at[b, 1], corner.at[b, 0], corner.at[b, 1]])
        new = dot(dot(const["late"][...], new).astype(BF16), wqkv2[:, DIM:])
        for a in range(2):
            keyval[b, a, pl.ds(pl.multiple_of(72 * (1 - b), 8), 72), :] = new[72 * a : 72 * a + 72]
        parts = []
        for a in range(2):
            khi, klo = split(keyval[b, a, :, :DIM])
            val = keyval[b, a, :, DIM:].astype(BF16)
            at = pl.ds(TOK * a, TOK)
            parts.append(
                attend(ahi[b, at], alo[b, at], khi, klo, val, lambda g, a=a: bias2[a, b, g], HALF)
            )
        return dot(const["fold2"][b], jnp.concatenate(parts, axis=0))

    unpack[...] = jnp.zeros_like(unpack)
    window_bias(1, tab2)
    get("wqkv2")
    qhi, qlo = split(dot(normed, wqkv2[:, :DIM]) * scale)
    get("rep2")
    rep = const["rep2"][...]
    ahi[...] = masked(dot(rep, qhi), HALF).reshape(2, 288, DIM)
    alo[...] = masked(dot(rep, qlo), HALF).reshape(2, 288, DIM)
    get("back")
    residual = dot(const["back"][...], first)
    get("early")
    get("late")
    get("fold2")
    get("wproj2")

    relay(side_near)

    @pl.when(jnp.logical_not(border))
    def _():
        relay(side_far)

    remote(tab2, tabn, tab_send, tab_recv, (south, lon)).wait_recv()
    window_bias(0, tabn)
    for a, has in ((0, has_n), (1, has_s)):
        @pl.when(has)
        def _(a=a):
            remote(packed.at[a], halo_lat.at[a], lat_send.at[a], lat_recv.at[a], (north, lon)).wait_recv()

    known = jnp.concatenate(
        [own[...], tokens_of([halo_lat.at[0, 0], halo_lat.at[0, 1], halo_lat.at[1, 0], halo_lat.at[1, 1]])], axis=0
    )
    known = dot(dot(const["early"][...], known).astype(BF16), wqkv2[:, DIM:])
    for b in range(2):
        for a in range(2):
            at = 144 * b + 72 * a
            keyval[b, a, 72 * b : 72 * b + 72, :] = known[at : at + 72]

    settle(side_near)
    near[...] = side(side_near)

    @pl.when(border)
    def _():
        relay(side_far)

    settle(side_far)
    heads = (near[...] + side(side_far)).astype(BF16)
    mixed = (residual + dot(heads, wproj2[...])).astype(BF16)
    for r in range(WIN):
        tok[0, r] = mixed[16 * r : 16 * r + WIN]
    store = pltpu.make_async_copy(tok, out_h, out_sem)
    store.start()

    for b in range(2):
        for a in range(2):
            edge(b, a).wait_send()
    send_tab.wait_send()
    for a, has, copy, peer in ((0, has_n, to_n, north), (1, has_s, to_s, south)):
        @pl.when(has)
        def _(a=a, copy=copy, peer=peer):
            copy.wait_send()
            for b in range(2):
                remote(
                    halo_lon.at[b, a], corner.at[b, 1 - a], cor_send.at[b, a], cor_recv.at[b, 1 - a], (peer, lon)
                ).wait_send()

    store.wait()


def shards(tokens, gain1, wqkv1, wproj1, bias1, gain2, wqkv2, wproj2, bias2):
    nlat = lax.axis_size("lat")
    nlon = lax.axis_size("lon")
    consts = [jnp.asarray(CONSTS[name], BF16) for name in CNAMES]
    dma = pltpu.SemaphoreType.DMA
    vmem = pltpu.VMEM
    args = [tokens, gain1.reshape(1, DIM), wqkv1, wproj1, bias1, gain2.reshape(1, DIM), wqkv2, wproj2, bias2]
    scratch = [vmem(x.shape, x.dtype) for x in args] + [vmem(bias2.shape, F32)]
    scratch += [vmem(x.shape, BF16) for x in consts]
    scratch += [
        vmem((192, DIM), BF16),
        vmem((HEADS, 640), F32),
        vmem((4, 576, TOK), F32),
        vmem((2, 2, 4, TOK, TOK), F32),
        vmem((192, DIM), F32),
        vmem((2, 2, TOK, 128), BF16),
        vmem((2, 2, TOK, 128), BF16),
        vmem((2, 2, TOK, 128), BF16),
        vmem((TOK, DIM), BF16),
        vmem((2, 2, TOK, 128), F32),
        vmem((2, 2, TOK, 128), BF16),
        vmem((160, DIM), F32),
        vmem((2, 2, TOK, 2 * DIM), F32),
        vmem((2, 288, DIM), BF16),
        vmem((2, 288, DIM), BF16),
        dma((len(args) + len(consts),)),
        dma(()),
        dma((2, 2)), dma((2, 2)),
        dma((2,)), dma((2,)),
        dma((2, 2)), dma((2, 2)),
        dma(()), dma(()),
    ]
    anywhere = pl.BlockSpec(memory_space=pl.ANY)
    return pl.pallas_call(
        functools.partial(kernel, nlat, nlon),
        out_shape=jax.ShapeDtypeStruct(tokens.shape, BF16),
        in_specs=[anywhere] * (len(args) + len(consts)),
        out_specs=anywhere,
        scratch_shapes=scratch,
        compiler_params=pltpu.CompilerParams(
            collective_id=0, has_side_effects=True, vmem_limit_bytes=62 * 1024 * 1024
        ),
        cost_estimate=pl.CostEstimate(flops=2_000_000_000, bytes_accessed=8_000_000, transcendentals=700_000),
        name="pair",
    )(*args, *consts)


def solution(mesh):
    placed = (
        P(None, "lat", "lon", None), P(), P(), P(), P("lat", None, None), P(), P(), P(), P("lat", None, None),
    )
    return jax.shard_map(
        shards, mesh=mesh, in_specs=placed, out_specs=P(None, "lat", "lon", None), check_vma=False
    )
```

```python
import functools
import math

import jax
import jax.numpy as jnp
import numpy as np
from jax import lax
from jax.experimental import pallas as pl
from jax.experimental.pallas import tpu as pltpu
from jax.sharding import PartitionSpec as P

HEADS = 16
WIN = 12
HALF = 6
TOK = 144
DIM = 512
LOG2E = math.log2(math.e)
MESH = pl.DeviceIdType.MESH
F32 = jnp.float32
BF16 = jnp.bfloat16


def own_at(r, c):
    return (c // HALF) * 72 + (r // HALF) * 36 + (r % HALF) * HALF + c % HALF


def constants():
    p0 = np.zeros((288, 192), np.float32)
    back = np.zeros((192, TOK), np.float32)
    rep = np.zeros((576, TOK), np.float32)
    fold = np.zeros((TOK, 576), np.float32)
    for r in range(WIN):
        for c in range(WIN):
            flipped = 143 - (c * WIN + r)
            p0[own_at(r, c), r * 16 + c] = 1
            p0[TOK + flipped, r * 16 + c] = 1
            back[r * 16 + c, own_at(r, c)] = 1
            for h in range(4):
                rep[c * 48 + h * WIN + r, flipped] = 1
                fold[own_at(r, c), c * 48 + h * WIN + r] = 1
    rep2 = np.zeros((576, TOK), np.float32)
    fold2 = np.zeros((2, 192, 288), np.float32)
    early = np.zeros((288, 304), np.float32)
    late = np.zeros((TOK, 160), np.float32)
    for b in range(2):
        for a in range(2):
            for c in range(HALF):
                for r in range(HALF):
                    at = r * HALF + c
                    for h in range(4):
                        row = a * TOK + c * 24 + h * HALF + r
                        rep2[b * 288 + row, b * 72 + a * 36 + at] = 1
                        fold2[b, (a * HALF + r) * 16 + b * HALF + c, row] = 1
                    for whole in (r, r + HALF):
                        key = (HALF - 1 - c) * WIN + WIN - 1 - whole
                        mine = (whole >= HALF) == (a == 0)
                        src = b * 72 + a * 36 + at if mine else 144 + 40 * (2 * a + b) + at
                        early[b * 144 + a * 72 + key, src] = 1
                        late[a * 72 + key, 40 * a + at if mine else 80 + 40 * a + at] = 1
    pick = np.zeros((384, 384), np.float32)
    for v in range(23):
        for r in range(WIN):
            pick[r * 23 + v, v * WIN + r] = 1
    order1 = np.zeros((192, 192), np.float32)
    order2 = np.zeros((96, 96), np.float32)
    for h in range(HEADS):
        for r in range(WIN):
            order1[h * WIN + r, r * HEADS + h] = 1
        for r in range(HALF):
            order2[h * HALF + r, r * HEADS + h] = 1
    return {
        "p0": p0,
        "pick": pick,
        "order1": np.concatenate([order1, order1], axis=1),
        "rep": rep,
        "fold": fold,
        "back": back,
        "order2": np.concatenate([order2, order2], axis=1),
        "rep2": rep2,
        "early": early,
        "late": late,
        "fold2": fold2,
    }


CONSTS = constants()
CNAMES = list(CONSTS)


def dot(a, b):
    return jnp.dot(a, b, preferred_element_type=F32)


def dot_nt(a, b):
    return lax.dot_general(a, b, (((1,), (1,)), ((), ())), preferred_element_type=F32)


def norm(data, gain):
    mean = jnp.mean(data, axis=-1, keepdims=True)
    centred = data - mean
    var = jnp.mean(centred * centred, axis=-1, keepdims=True)
    return (centred * lax.rsqrt(var + 1e-05) * gain).astype(BF16)


def split(values):
    high = values.astype(BF16)
    return high, (values - high.astype(F32)).astype(BF16)


def head_mask(size, width):
    row = lax.broadcasted_iota(jnp.int32, (4 * size, width), 0)
    lane = lax.broadcasted_iota(jnp.int32, (4 * size, width), 1)
    head = (row >= size).astype(jnp.int32) + (row >= 2 * size).astype(jnp.int32) + (row >= 3 * size).astype(jnp.int32)
    return head == ((lane // 32) & 3)


def masked(values, size):
    rows, width = values.shape
    mask = head_mask(size, width)
    kept = jnp.where(mask[None], values.reshape(rows // (4 * size), 4 * size, width), 0.0)
    return kept.reshape(rows, width).astype(BF16)


def offsets_table(table, padded, pick, order, start, count):
    padded[...] = jnp.zeros_like(padded)
    padded[:, :529] = table
    flat = padded[...] * LOG2E
    moved = [pltpu.roll(flat, (640 - 23 * r) % 640, 1) if r else flat for r in range(start, start + count)]
    rows = jnp.concatenate([m[:, :384] for m in moved], axis=0)
    high, low = split(rows)
    parts = jnp.concatenate([dot(high, pick).astype(BF16), dot(low, pick).astype(BF16)], axis=0)
    return dot(order, parts)


def attend(windows, size):
    units = [(w, slice(128 * g, 128 * g + 128), g) for w in windows for g in range(4)]
    ones = jnp.ones((TOK, 128), BF16)
    scores = []
    for (qhi, qlo, khi, klo, _, bias), at, g in units:
        left = jnp.concatenate([qhi[:, at], qlo[:, at], qhi[:, at]], axis=1)
        right = jnp.concatenate([khi[:, at], khi[:, at], klo[:, at]], axis=1)
        scores.append(dot_nt(left, right) + bias(g))
    expo = [jnp.exp2(x - jnp.max(x, axis=-1, keepdims=True)).astype(BF16) for x in scores]
    both = [dot(e, jnp.concatenate([w[4][:, at], ones], axis=1)) for e, (w, at, _) in zip(expo, units)]
    parts = [masked(x[:, :128] / x[:, 128:], size) for x in both]
    return [jnp.concatenate(parts[4 * i : 4 * i + 4], axis=1) for i in range(len(windows))]


def kernel(
    nlat, nlon, tok_h, gain1_h, wqkv1_h, wproj1_h, bias1_h, gain2_h, wqkv2_h, wproj2_h, bias2_h, *rest
):
    nc = len(CNAMES)
    const_h = dict(zip(CNAMES, rest[:nc]))
    out_h = rest[nc]
    (tok, gain1, wqkv1, wproj1, tab1, gain2, wqkv2, wproj2, tab2, tabn), rest = rest[nc + 1 : nc + 11], rest[nc + 11 :]
    const = dict(zip(CNAMES, rest[:nc]))
    (
        xpad, tpad, bias1, bias2, near, halo_lon, halo_lat, corner, own, pack, packed, unpack, keyval, ahi, alo,
        in_sem, out_sem, lon_send, lon_recv, lat_send, lat_recv, cor_send, cor_recv, tab_send, tab_recv,
    ) = rest[nc:]

    lat = lax.axis_index("lat")
    lon = lax.axis_index("lon")
    north = lax.rem(lat + nlat - 1, nlat)
    south = lax.rem(lat + 1, nlat)
    west = lax.rem(lon + nlon - 1, nlon)
    east = lax.rem(lon + 1, nlon)
    has_n = lat > 0
    has_s = lat < nlat - 1

    barrier = pltpu.get_barrier_semaphore()
    for peer in ((lat, west), (lat, east), (north, lon), (south, lon)):
        pl.semaphore_signal(barrier, inc=1, device_id=peer, device_id_type=MESH)

    loads = {}
    early_loads = [
        ("tab1", bias1_h, tab1), ("pick", const_h["pick"], const["pick"]), ("order1", const_h["order1"], const["order1"]),
        ("tok", tok_h, tok), ("p0", const_h["p0"], const["p0"]), ("gain1", gain1_h, gain1),
        ("wqkv1", wqkv1_h, wqkv1), ("rep", const_h["rep"], const["rep"]), ("fold", const_h["fold"], const["fold"]),
        ("wproj1", wproj1_h, wproj1), ("gain2", gain2_h, gain2), ("tab2", bias2_h, tab2),
    ]
    late_loads = [
        ("order2", const_h["order2"], const["order2"]), ("wqkv2", wqkv2_h, wqkv2), ("rep2", const_h["rep2"], const["rep2"]),
        ("back", const_h["back"], const["back"]), ("early", const_h["early"], const["early"]),
        ("late", const_h["late"], const["late"]), ("fold2", const_h["fold2"], const["fold2"]), ("wproj2", wproj2_h, wproj2),
    ]
    for i, (name, src, dst) in enumerate(early_loads + late_loads):
        loads[name] = pltpu.make_async_copy(src, dst, in_sem.at[i])
    for name, _, _ in early_loads:
        loads[name].start()

    def get(name):
        loads[name].wait()

    get("tab1")
    get("pick")
    get("order1")
    table = offsets_table(tab1[0], tpad, const["pick"][...], const["order1"][...], 0, WIN)
    for c in range(WIN):
        moved = table[:, WIN * c : WIN * c + TOK]
        for g in range(4):
            bias1[g, 48 * c : 48 * c + 48, :] = moved[48 * g : 48 * g + 48]

    get("tok")
    get("p0")
    xpad[...] = jnp.zeros_like(xpad)
    for r in range(WIN):
        xpad[16 * r : 16 * r + WIN, :] = tok[0, r]
    both = dot(const["p0"][...], xpad[...])
    mine = both[:TOK]
    get("gain1")
    normed = norm(both[TOK:], gain1[...])
    get("wqkv1")
    scale = LOG2E / math.sqrt(32.0)
    flat = dot(normed, wqkv1[...])
    qhi, qlo = split(flat[:, :DIM] * scale)
    khi, klo = split(flat[:, DIM : 2 * DIM])
    val = flat[:, 2 * DIM :].astype(BF16)
    get("rep")
    for name, _, _ in late_loads:
        loads[name].start()
    rep = const["rep"][...]
    (heads,) = attend(
        [(masked(dot(rep, qhi), WIN), masked(dot(rep, qlo), WIN), khi, klo, val, lambda g: bias1[g])], WIN
    )
    get("fold")
    get("wproj1")
    heads = dot(const["fold"][...], heads).astype(BF16)
    first = (mine + dot(heads, wproj1[...])).astype(BF16)
    get("gain2")
    normed = norm(first.astype(F32), gain2[...])
    own[...] = normed
    wide = normed.astype(F32)
    for a in range(2):
        for b in range(2):
            for j in range(4):
                at = 72 * b + 36 * a
                pack[a, b, 36 * j : 36 * j + 36, :] = wide[at : at + 36, 128 * j : 128 * j + 128]
    packed[...] = pack[...].astype(BF16)

    side_far = jnp.where(lax.rem(lon, nlon // 2) == 0, 0, 1)
    side_near = 1 - side_far
    border = jnp.logical_or(lax.rem(lon, nlon // 2) == 0, lax.rem(lon, nlon // 2) == nlon // 2 - 1)
    part0 = lax.rem(lat, 2)
    get("tab2")
    pl.semaphore_wait(barrier, 4)

    def remote(src, dst, send, recv, peer):
        return pltpu.make_async_remote_copy(
            src_ref=src, dst_ref=dst, send_sem=send, recv_sem=recv, device_id=peer, device_id_type=MESH
        )

    def edge(b, a):
        peer = jnp.where(b == 0, west, east)
        return remote(packed.at[a, b], halo_lon.at[1 - b, a], lon_send.at[b, a], lon_recv.at[1 - b, a], (lat, peer))

    for b in (side_far, side_near):
        for a in (part0, 1 - part0):
            edge(b, a).start()
    to_n = remote(packed.at[0], halo_lat.at[1], lat_send.at[0], lat_recv.at[1], (north, lon))
    to_s = remote(packed.at[1], halo_lat.at[0], lat_send.at[1], lat_recv.at[0], (south, lon))

    @pl.when(has_n)
    def _():
        to_n.start()

    @pl.when(has_s)
    def _():
        to_s.start()

    send_tab = remote(tab2, tabn, tab_send, tab_recv, (south, lon))
    send_tab.start()

    for a, has in ((0, has_n), (1, has_s)):
        @pl.when(jnp.logical_not(has))
        def _(a=a):
            halo_lat[a] = jnp.zeros((2, TOK, 128), BF16)
            for b in range(2):
                corner[b, a] = jnp.zeros((TOK, 128), BF16)

    get("order2")

    def window_bias(a, ref):
        start = HALF if a == 0 else 0
        table = offsets_table(ref[0], tpad, const["pick"][...], const["order2"][...], start, HALF)
        cut = jnp.logical_not(has_n if a == 0 else has_s)
        lane = lax.rem(lax.broadcasted_iota(jnp.int32, (1, TOK), 1), WIN)
        other = (lane >= HALF) if a == 0 else (lane < HALF)
        shut = jnp.where(other, jnp.where(cut, -1e30, 0.0), 0.0)
        for c in range(WIN):
            moved = table[:, WIN * c : WIN * c + TOK] + shut
            b = 0 if c >= HALF else 1
            row = 24 * (c % HALF)
            for g in range(4):
                bias2[a, b, g, row : row + 24, :] = moved[24 * g : 24 * g + 24]

    def relay(b):
        for a in (part0, 1 - part0):
            remote(packed.at[a, b], halo_lon.at[b, a], lon_send.at[b, a], lon_recv.at[b, a], (lat, west)).wait_recv()
            peer = jnp.where(a == 0, north, south)

            @pl.when(jnp.where(a == 0, lat > 0, lat < nlat - 1))
            def _(a=a, peer=peer):
                remote(
                    halo_lon.at[b, a], corner.at[b, 1 - a], cor_send.at[b, a], cor_recv.at[b, 1 - a], (peer, lon)
                ).start()

    def settle(b):
        for a, has in ((0, has_n), (1, has_s)):
            @pl.when(has)
            def _(a=a):
                remote(
                    halo_lon.at[b, a], corner.at[b, a], cor_send.at[b, a], cor_recv.at[b, a], (north, lon)
                ).wait_recv()

    def tokens_of(quadrants):
        for i, ref in enumerate(quadrants):
            data = ref[...].astype(F32)
            for j in range(4):
                unpack[40 * i : 40 * i + 36, 128 * j : 128 * j + 128] = data[36 * j : 36 * j + 36]
        return unpack[...].astype(BF16)

    def side(b):
        new = tokens_of([halo_lon.at[b, 0], halo_lon.at[b, 1], corner.at[b, 0], corner.at[b, 1]])
        new = dot(dot(const["late"][...], new).astype(BF16), wqkv2[:, DIM:])
        for a in range(2):
            keyval[b, a, pl.ds(pl.multiple_of(72 * (1 - b), 8), 72), :] = new[72 * a : 72 * a + 72]
        windows = []
        for a in range(2):
            khi, klo = split(keyval[b, a, :, :DIM])
            val = keyval[b, a, :, DIM:].astype(BF16)
            at = pl.ds(TOK * a, TOK)
            windows.append((ahi[b, at], alo[b, at], khi, klo, val, lambda g, a=a: bias2[a, b, g]))
        return dot(const["fold2"][b], jnp.concatenate(attend(windows, HALF), axis=0))

    unpack[...] = jnp.zeros_like(unpack)
    window_bias(1, tab2)
    get("wqkv2")
    qhi, qlo = split(dot(normed, wqkv2[:, :DIM]) * scale)
    get("rep2")
    rep = const["rep2"][...]
    ahi[...] = masked(dot(rep, qhi), HALF).reshape(2, 288, DIM)
    alo[...] = masked(dot(rep, qlo), HALF).reshape(2, 288, DIM)
    get("back")
    residual = dot(const["back"][...], first)
    get("early")
    get("late")
    get("fold2")
    get("wproj2")

    relay(side_near)

    @pl.when(jnp.logical_not(border))
    def _():
        relay(side_far)

    remote(tab2, tabn, tab_send, tab_recv, (south, lon)).wait_recv()
    window_bias(0, tabn)
    for a, has in ((0, has_n), (1, has_s)):
        @pl.when(has)
        def _(a=a):
            remote(packed.at[a], halo_lat.at[a], lat_send.at[a], lat_recv.at[a], (north, lon)).wait_recv()

    known = jnp.concatenate(
        [own[...], tokens_of([halo_lat.at[0, 0], halo_lat.at[0, 1], halo_lat.at[1, 0], halo_lat.at[1, 1]])], axis=0
    )
    known = dot(dot(const["early"][...], known).astype(BF16), wqkv2[:, DIM:])
    for b in range(2):
        for a in range(2):
            at = 144 * b + 72 * a
            keyval[b, a, 72 * b : 72 * b + 72, :] = known[at : at + 72]

    settle(side_near)
    near[...] = side(side_near)

    @pl.when(border)
    def _():
        relay(side_far)

    settle(side_far)
    heads = (near[...] + side(side_far)).astype(BF16)
    mixed = (residual + dot(heads, wproj2[...])).astype(BF16)
    for r in range(WIN):
        tok[0, r] = mixed[16 * r : 16 * r + WIN]
    store = pltpu.make_async_copy(tok, out_h, out_sem)
    store.start()

    for b in range(2):
        for a in range(2):
            edge(b, a).wait_send()
    send_tab.wait_send()
    for a, has, copy, peer in ((0, has_n, to_n, north), (1, has_s, to_s, south)):
        @pl.when(has)
        def _(a=a, copy=copy, peer=peer):
            copy.wait_send()
            for b in range(2):
                remote(
                    halo_lon.at[b, a], corner.at[b, 1 - a], cor_send.at[b, a], cor_recv.at[b, 1 - a], (peer, lon)
                ).wait_send()

    store.wait()


def shards(tokens, gain1, wqkv1, wproj1, bias1, gain2, wqkv2, wproj2, bias2):
    nlat = lax.axis_size("lat")
    nlon = lax.axis_size("lon")
    consts = [jnp.asarray(CONSTS[name], BF16) for name in CNAMES]
    dma = pltpu.SemaphoreType.DMA
    vmem = pltpu.VMEM
    args = [tokens, gain1.reshape(1, DIM), wqkv1, wproj1, bias1, gain2.reshape(1, DIM), wqkv2, wproj2, bias2]
    scratch = [vmem(x.shape, x.dtype) for x in args] + [vmem(bias2.shape, F32)]
    scratch += [vmem(x.shape, BF16) for x in consts]
    scratch += [
        vmem((192, DIM), BF16),
        vmem((HEADS, 640), F32),
        vmem((4, 576, TOK), F32),
        vmem((2, 2, 4, TOK, TOK), F32),
        vmem((192, DIM), F32),
        vmem((2, 2, TOK, 128), BF16),
        vmem((2, 2, TOK, 128), BF16),
        vmem((2, 2, TOK, 128), BF16),
        vmem((TOK, DIM), BF16),
        vmem((2, 2, TOK, 128), F32),
        vmem((2, 2, TOK, 128), BF16),
        vmem((160, DIM), F32),
        vmem((2, 2, TOK, 2 * DIM), F32),
        vmem((2, 288, DIM), BF16),
        vmem((2, 288, DIM), BF16),
        dma((len(args) + len(consts),)),
        dma(()),
        dma((2, 2)), dma((2, 2)),
        dma((2,)), dma((2,)),
        dma((2, 2)), dma((2, 2)),
        dma(()), dma(()),
    ]
    anywhere = pl.BlockSpec(memory_space=pl.ANY)
    return pl.pallas_call(
        functools.partial(kernel, nlat, nlon),
        out_shape=jax.ShapeDtypeStruct(tokens.shape, BF16),
        in_specs=[anywhere] * (len(args) + len(consts)),
        out_specs=anywhere,
        scratch_shapes=scratch,
        compiler_params=pltpu.CompilerParams(
            collective_id=0, has_side_effects=True, vmem_limit_bytes=62 * 1024 * 1024
        ),
        cost_estimate=pl.CostEstimate(flops=2_000_000_000, bytes_accessed=8_000_000, transcendentals=700_000),
        name="pair",
    )(*args, *consts)


def solution(mesh):
    placed = (
        P(None, "lat", "lon", None), P(), P(), P(), P("lat", None, None), P(), P(), P(), P("lat", None, None),
    )
    return jax.shard_map(
        shards, mesh=mesh, in_specs=placed, out_specs=P(None, "lat", "lon", None), check_vma=False
    )
```

```python
import functools
import math

import jax
import jax.numpy as jnp
import numpy as np
from jax import lax
from jax.experimental import pallas as pl
from jax.experimental.pallas import tpu as pltpu
from jax.sharding import PartitionSpec as P

HEADS = 16
WIN = 12
HALF = 6
TOK = 144
DIM = 512
LOG2E = math.log2(math.e)
MESH = pl.DeviceIdType.MESH
F32 = jnp.float32
BF16 = jnp.bfloat16


def own_at(r, c):
    return (c // HALF) * 72 + (r // HALF) * 36 + (r % HALF) * HALF + c % HALF


def constants():
    p0 = np.zeros((288, 192), np.float32)
    back = np.zeros((192, TOK), np.float32)
    rep = np.zeros((576, TOK), np.float32)
    fold = np.zeros((TOK, 576), np.float32)
    for r in range(WIN):
        for c in range(WIN):
            flipped = 143 - (c * WIN + r)
            p0[own_at(r, c), r * 16 + c] = 1
            p0[TOK + flipped, r * 16 + c] = 1
            back[r * 16 + c, own_at(r, c)] = 1
            for h in range(4):
                rep[c * 48 + h * WIN + r, flipped] = 1
                fold[own_at(r, c), c * 48 + h * WIN + r] = 1
    rep2 = np.zeros((576, TOK), np.float32)
    fold2 = np.zeros((2, 192, 288), np.float32)
    early = np.zeros((288, 304), np.float32)
    late = np.zeros((TOK, 160), np.float32)
    for b in range(2):
        for a in range(2):
            for c in range(HALF):
                for r in range(HALF):
                    at = r * HALF + c
                    for h in range(4):
                        row = a * TOK + c * 24 + h * HALF + r
                        rep2[b * 288 + row, b * 72 + a * 36 + at] = 1
                        fold2[b, (a * HALF + r) * 16 + b * HALF + c, row] = 1
                    for whole in (r, r + HALF):
                        key = (HALF - 1 - c) * WIN + WIN - 1 - whole
                        mine = (whole >= HALF) == (a == 0)
                        src = b * 72 + a * 36 + at if mine else 144 + 40 * (2 * a + b) + at
                        early[b * 144 + a * 72 + key, src] = 1
                        late[a * 72 + key, 40 * a + at if mine else 80 + 40 * a + at] = 1
    pick = np.zeros((384, 384), np.float32)
    for v in range(23):
        for r in range(WIN):
            pick[r * 23 + v, v * WIN + r] = 1
    order1 = np.zeros((192, 192), np.float32)
    order2 = np.zeros((96, 96), np.float32)
    for h in range(HEADS):
        for r in range(WIN):
            order1[h * WIN + r, r * HEADS + h] = 1
        for r in range(HALF):
            order2[h * HALF + r, r * HEADS + h] = 1
    return {
        "p0": p0,
        "pick": pick,
        "order1": np.concatenate([order1, order1], axis=1),
        "rep": rep,
        "fold": fold,
        "back": back,
        "order2": np.concatenate([order2, order2], axis=1),
        "rep2": rep2,
        "early": early,
        "late": late,
        "fold2": fold2,
    }


CONSTS = constants()
CNAMES = list(CONSTS)


def dot(a, b):
    return jnp.dot(a, b, preferred_element_type=F32)


def dot_nt(a, b):
    return lax.dot_general(a, b, (((1,), (1,)), ((), ())), preferred_element_type=F32)


def norm(data, gain):
    mean = jnp.mean(data, axis=-1, keepdims=True)
    centred = data - mean
    var = jnp.mean(centred * centred, axis=-1, keepdims=True)
    return (centred * lax.rsqrt(var + 1e-05) * gain).astype(BF16)


def split(values):
    high = values.astype(BF16)
    return high, (values - high.astype(F32)).astype(BF16)


def head_mask(size, width):
    row = lax.broadcasted_iota(jnp.int32, (4 * size, width), 0)
    lane = lax.broadcasted_iota(jnp.int32, (4 * size, width), 1)
    head = (row >= size).astype(jnp.int32) + (row >= 2 * size).astype(jnp.int32) + (row >= 3 * size).astype(jnp.int32)
    return head == ((lane // 32) & 3)


def masked(values, size):
    rows, width = values.shape
    mask = head_mask(size, width)
    kept = jnp.where(mask[None], values.reshape(rows // (4 * size), 4 * size, width), 0.0)
    return kept.reshape(rows, width).astype(BF16)


def offsets_table(table, padded, pick, order, start, count):
    padded[...] = jnp.zeros_like(padded)
    padded[:, :529] = table
    flat = padded[...] * LOG2E
    moved = [pltpu.roll(flat, (640 - 23 * r) % 640, 1) if r else flat for r in range(start, start + count)]
    rows = jnp.concatenate([m[:, :384] for m in moved], axis=0)
    high, low = split(rows)
    parts = jnp.concatenate([dot(high, pick).astype(BF16), dot(low, pick).astype(BF16)], axis=0)
    return dot(order, parts)


def attend(windows, size):
    units = [(w, slice(128 * g, 128 * g + 128), g) for w in windows for g in range(4)]
    ones = jnp.ones((TOK, 128), BF16)
    scores = []
    for (qhi, qlo, khi, klo, _, bias), at, g in units:
        left = jnp.concatenate([qhi[:, at], qlo[:, at], qhi[:, at]], axis=1)
        right = jnp.concatenate([khi[:, at], khi[:, at], klo[:, at]], axis=1)
        scores.append(dot_nt(left, right) + bias(g))
    expo = [jnp.exp2(x - jnp.max(x, axis=-1, keepdims=True)).astype(BF16) for x in scores]
    both = [dot(e, jnp.concatenate([w[4][:, at], ones], axis=1)) for e, (w, at, _) in zip(expo, units)]
    parts = [masked(x[:, :128] / x[:, 128:], size) for x in both]
    return [jnp.concatenate(parts[4 * i : 4 * i + 4], axis=1) for i in range(len(windows))]


def kernel(
    nlat, nlon, tok_h, gain1_h, wqkv1_h, wproj1_h, bias1_h, gain2_h, wqkv2_h, wproj2_h, bias2_h, *rest
):
    nc = len(CNAMES)
    const_h = dict(zip(CNAMES, rest[:nc]))
    out_h = rest[nc]
    (tok, gain1, wqkv1, wproj1, tab1, gain2, wqkv2, wproj2, tab2, tabn), rest = rest[nc + 1 : nc + 11], rest[nc + 11 :]
    const = dict(zip(CNAMES, rest[:nc]))
    (
        xpad, tpad, bias1, bias2, near, halo_lon, halo_lat, corner, own, pack, packed, unpack, keyval, ahi, alo,
        in_sem, out_sem, lon_send, lon_recv, lat_send, lat_recv, cor_send, cor_recv, tab_send, tab_recv,
    ) = rest[nc:]

    lat = lax.axis_index("lat")
    lon = lax.axis_index("lon")
    north = lax.rem(lat + nlat - 1, nlat)
    south = lax.rem(lat + 1, nlat)
    west = lax.rem(lon + nlon - 1, nlon)
    east = lax.rem(lon + 1, nlon)
    has_n = lat > 0
    has_s = lat < nlat - 1

    barrier = pltpu.get_barrier_semaphore()
    for peer in ((lat, west), (lat, east), (north, lon), (south, lon)):
        pl.semaphore_signal(barrier, inc=1, device_id=peer, device_id_type=MESH)

    loads = {}
    early_loads = [
        ("tab1", bias1_h, tab1), ("pick", const_h["pick"], const["pick"]), ("order1", const_h["order1"], const["order1"]),
        ("tok", tok_h, tok), ("p0", const_h["p0"], const["p0"]), ("gain1", gain1_h, gain1),
        ("wqkv1", wqkv1_h, wqkv1), ("rep", const_h["rep"], const["rep"]), ("fold", const_h["fold"], const["fold"]),
        ("wproj1", wproj1_h, wproj1), ("gain2", gain2_h, gain2), ("tab2", bias2_h, tab2),
    ]
    late_loads = [
        ("order2", const_h["order2"], const["order2"]), ("wqkv2", wqkv2_h, wqkv2), ("rep2", const_h["rep2"], const["rep2"]),
        ("back", const_h["back"], const["back"]), ("early", const_h["early"], const["early"]),
        ("late", const_h["late"], const["late"]), ("fold2", const_h["fold2"], const["fold2"]), ("wproj2", wproj2_h, wproj2),
    ]
    for i, (name, src, dst) in enumerate(early_loads + late_loads):
        loads[name] = pltpu.make_async_copy(src, dst, in_sem.at[i])
    for name, _, _ in early_loads:
        loads[name].start()

    def get(name):
        loads[name].wait()

    get("tab1")
    get("pick")
    get("order1")
    table = offsets_table(tab1[0], tpad, const["pick"][...], const["order1"][...], 0, WIN)
    for c in range(WIN):
        moved = table[:, WIN * c : WIN * c + TOK]
        for g in range(4):
            bias1[g, 48 * c : 48 * c + 48, :] = moved[48 * g : 48 * g + 48]

    get("tok")
    get("p0")
    xpad[...] = jnp.zeros_like(xpad)
    for r in range(WIN):
        xpad[16 * r : 16 * r + WIN, :] = tok[0, r]
    both = dot(const["p0"][...], xpad[...])
    mine = both[:TOK]
    get("gain1")
    normed = norm(both[TOK:], gain1[...])
    get("wqkv1")
    scale = LOG2E / math.sqrt(32.0)
    flat = dot(normed, wqkv1[...])
    qhi, qlo = split(flat[:, :DIM] * scale)
    khi, klo = split(flat[:, DIM : 2 * DIM])
    val = flat[:, 2 * DIM :].astype(BF16)
    get("rep")
    for name, _, _ in late_loads:
        loads[name].start()
    rep = const["rep"][...]
    (heads,) = attend(
        [(masked(dot(rep, qhi), WIN), masked(dot(rep, qlo), WIN), khi, klo, val, lambda g: bias1[g])], WIN
    )
    get("fold")
    get("wproj1")
    heads = dot(const["fold"][...], heads).astype(BF16)
    first = (mine + dot(heads, wproj1[...])).astype(BF16)
    get("gain2")
    normed = norm(first.astype(F32), gain2[...])
    own[...] = normed
    wide = normed.astype(F32)
    for a in range(2):
        for b in range(2):
            for j in range(4):
                at = 72 * b + 36 * a
                pack[a, b, 36 * j : 36 * j + 36, :] = wide[at : at + 36, 128 * j : 128 * j + 128]
    packed[...] = pack[...].astype(BF16)

    side_far = jnp.where(lax.rem(lon, nlon // 2) == 0, 0, 1)
    side_near = 1 - side_far
    border = jnp.logical_or(lax.rem(lon, nlon // 2) == 0, lax.rem(lon, nlon // 2) == nlon // 2 - 1)
    part0 = lax.rem(lat, 2)
    get("tab2")
    pl.semaphore_wait(barrier, 4)

    def remote(src, dst, send, recv, peer):
        return pltpu.make_async_remote_copy(
            src_ref=src, dst_ref=dst, send_sem=send, recv_sem=recv, device_id=peer, device_id_type=MESH
        )

    def edge(b, a):
        peer = jnp.where(b == 0, west, east)
        return remote(packed.at[a, b], halo_lon.at[1 - b, a], lon_send.at[b, a], lon_recv.at[1 - b, a], (lat, peer))

    edge(side_far, part0).start()
    to_n = remote(packed.at[0], halo_lat.at[1], lat_send.at[0], lat_recv.at[1], (north, lon))
    to_s = remote(packed.at[1], halo_lat.at[0], lat_send.at[1], lat_recv.at[0], (south, lon))

    for a, has in ((0, has_n), (1, has_s)):
        @pl.when(jnp.logical_not(has))
        def _(a=a):
            halo_lat[a] = jnp.zeros((2, TOK, 128), BF16)
            for b in range(2):
                corner[b, a] = jnp.zeros((TOK, 128), BF16)

    get("order2")

    def window_bias(a, ref):
        start = HALF if a == 0 else 0
        table = offsets_table(ref[0], tpad, const["pick"][...], const["order2"][...], start, HALF)
        cut = jnp.logical_not(has_n if a == 0 else has_s)
        lane = lax.rem(lax.broadcasted_iota(jnp.int32, (1, TOK), 1), WIN)
        other = (lane >= HALF) if a == 0 else (lane < HALF)
        shut = jnp.where(other, jnp.where(cut, -1e30, 0.0), 0.0)
        for c in range(WIN):
            moved = table[:, WIN * c : WIN * c + TOK] + shut
            b = 0 if c >= HALF else 1
            row = 24 * (c % HALF)
            for g in range(4):
                bias2[a, b, g, row : row + 24, :] = moved[24 * g : 24 * g + 24]

    def relay(b):
        for a in (part0, 1 - part0):
            remote(packed.at[a, b], halo_lon.at[b, a], lon_send.at[b, a], lon_recv.at[b, a], (lat, west)).wait_recv()
            peer = jnp.where(a == 0, north, south)

            @pl.when(jnp.where(a == 0, lat > 0, lat < nlat - 1))
            def _(a=a, peer=peer):
                remote(
                    halo_lon.at[b, a], corner.at[b, 1 - a], cor_send.at[b, a], cor_recv.at[b, 1 - a], (peer, lon)
                ).start()

    def settle(b):
        for a, has in ((0, has_n), (1, has_s)):
            @pl.when(has)
            def _(a=a):
                remote(
                    halo_lon.at[b, a], corner.at[b, a], cor_send.at[b, a], cor_recv.at[b, a], (north, lon)
                ).wait_recv()

    def tokens_of(quadrants):
        for i, ref in enumerate(quadrants):
            data = ref[...].astype(F32)
            for j in range(4):
                unpack[40 * i : 40 * i + 36, 128 * j : 128 * j + 128] = data[36 * j : 36 * j + 36]
        return unpack[...].astype(BF16)

    def side(b):
        new = tokens_of([halo_lon.at[b, 0], halo_lon.at[b, 1], corner.at[b, 0], corner.at[b, 1]])
        new = dot(dot(const["late"][...], new).astype(BF16), wqkv2[:, DIM:])
        for a in range(2):
            keyval[b, a, pl.ds(pl.multiple_of(72 * (1 - b), 8), 72), :] = new[72 * a : 72 * a + 72]
        windows = []
        for a in range(2):
            khi, klo = split(keyval[b, a, :, :DIM])
            val = keyval[b, a, :, DIM:].astype(BF16)
            at = pl.ds(TOK * a, TOK)
            windows.append((ahi[b, at], alo[b, at], khi, klo, val, lambda g, a=a: bias2[a, b, g]))
        return dot(const["fold2"][b], jnp.concatenate(attend(windows, HALF), axis=0))

    unpack[...] = jnp.zeros_like(unpack)
    window_bias(1, tab2)
    get("wqkv2")
    qhi, qlo = split(dot(normed, wqkv2[:, :DIM]) * scale)
    get("rep2")
    rep = const["rep2"][...]
    ahi[...] = masked(dot(rep, qhi), HALF).reshape(2, 288, DIM)
    alo[...] = masked(dot(rep, qlo), HALF).reshape(2, 288, DIM)
    edge(side_far, 1 - part0).start()
    for a in (part0, 1 - part0):
        edge(side_near, a).start()
    @pl.when(has_n)
    def _():
        to_n.start()

    @pl.when(has_s)
    def _():
        to_s.start()

    send_tab = remote(tab2, tabn, tab_send, tab_recv, (south, lon))
    send_tab.start()

    get("back")
    residual = dot(const["back"][...], first)
    get("early")
    get("late")
    get("fold2")
    get("wproj2")

    relay(side_near)

    @pl.when(jnp.logical_not(border))
    def _():
        relay(side_far)

    remote(tab2, tabn, tab_send, tab_recv, (south, lon)).wait_recv()
    window_bias(0, tabn)
    for a, has in ((0, has_n), (1, has_s)):
        @pl.when(has)
        def _(a=a):
            remote(packed.at[a], halo_lat.at[a], lat_send.at[a], lat_recv.at[a], (north, lon)).wait_recv()

    known = jnp.concatenate(
        [own[...], tokens_of([halo_lat.at[0, 0], halo_lat.at[0, 1], halo_lat.at[1, 0], halo_lat.at[1, 1]])], axis=0
    )
    known = dot(dot(const["early"][...], known).astype(BF16), wqkv2[:, DIM:])
    for b in range(2):
        for a in range(2):
            at = 144 * b + 72 * a
            keyval[b, a, 72 * b : 72 * b + 72, :] = known[at : at + 72]

    settle(side_near)
    near[...] = side(side_near)

    @pl.when(border)
    def _():
        relay(side_far)

    settle(side_far)
    heads = (near[...] + side(side_far)).astype(BF16)
    mixed = (residual + dot(heads, wproj2[...])).astype(BF16)
    for r in range(WIN):
        tok[0, r] = mixed[16 * r : 16 * r + WIN]
    store = pltpu.make_async_copy(tok, out_h, out_sem)
    store.start()

    for b in range(2):
        for a in range(2):
            edge(b, a).wait_send()
    send_tab.wait_send()
    for a, has, copy, peer in ((0, has_n, to_n, north), (1, has_s, to_s, south)):
        @pl.when(has)
        def _(a=a, copy=copy, peer=peer):
            copy.wait_send()
            for b in range(2):
                remote(
                    halo_lon.at[b, a], corner.at[b, 1 - a], cor_send.at[b, a], cor_recv.at[b, 1 - a], (peer, lon)
                ).wait_send()

    store.wait()


def shards(tokens, gain1, wqkv1, wproj1, bias1, gain2, wqkv2, wproj2, bias2):
    nlat = lax.axis_size("lat")
    nlon = lax.axis_size("lon")
    consts = [jnp.asarray(CONSTS[name], BF16) for name in CNAMES]
    dma = pltpu.SemaphoreType.DMA
    vmem = pltpu.VMEM
    args = [tokens, gain1.reshape(1, DIM), wqkv1, wproj1, bias1, gain2.reshape(1, DIM), wqkv2, wproj2, bias2]
    scratch = [vmem(x.shape, x.dtype) for x in args] + [vmem(bias2.shape, F32)]
    scratch += [vmem(x.shape, BF16) for x in consts]
    scratch += [
        vmem((192, DIM), BF16),
        vmem((HEADS, 640), F32),
        vmem((4, 576, TOK), F32),
        vmem((2, 2, 4, TOK, TOK), F32),
        vmem((192, DIM), F32),
        vmem((2, 2, TOK, 128), BF16),
        vmem((2, 2, TOK, 128), BF16),
        vmem((2, 2, TOK, 128), BF16),
        vmem((TOK, DIM), BF16),
        vmem((2, 2, TOK, 128), F32),
        vmem((2, 2, TOK, 128), BF16),
        vmem((160, DIM), F32),
        vmem((2, 2, TOK, 2 * DIM), F32),
        vmem((2, 288, DIM), BF16),
        vmem((2, 288, DIM), BF16),
        dma((len(args) + len(consts),)),
        dma(()),
        dma((2, 2)), dma((2, 2)),
        dma((2,)), dma((2,)),
        dma((2, 2)), dma((2, 2)),
        dma(()), dma(()),
    ]
    anywhere = pl.BlockSpec(memory_space=pl.ANY)
    return pl.pallas_call(
        functools.partial(kernel, nlat, nlon),
        out_shape=jax.ShapeDtypeStruct(tokens.shape, BF16),
        in_specs=[anywhere] * (len(args) + len(consts)),
        out_specs=anywhere,
        scratch_shapes=scratch,
        compiler_params=pltpu.CompilerParams(
            collective_id=0, has_side_effects=True, vmem_limit_bytes=62 * 1024 * 1024
        ),
        cost_estimate=pl.CostEstimate(flops=2_000_000_000, bytes_accessed=8_000_000, transcendentals=700_000),
        name="pair",
    )(*args, *consts)


def solution(mesh):
    placed = (
        P(None, "lat", "lon", None), P(), P(), P(), P("lat", None, None), P(), P(), P(), P("lat", None, None),
    )
    return jax.shard_map(
        shards, mesh=mesh, in_specs=placed, out_specs=P(None, "lat", "lon", None), check_vma=False
    )
```

```python
import functools
import math

import jax
import jax.numpy as jnp
import numpy as np
from jax import lax
from jax.experimental import pallas as pl
from jax.experimental.pallas import tpu as pltpu
from jax.sharding import PartitionSpec as P

HEADS = 16
WIN = 12
HALF = 6
TOK = 144
DIM = 512
LOG2E = math.log2(math.e)
MESH = pl.DeviceIdType.MESH
F32 = jnp.float32
BF16 = jnp.bfloat16


def own_at(r, c):
    return (c // HALF) * 72 + (r // HALF) * 36 + (r % HALF) * HALF + c % HALF


def constants():
    p0 = np.zeros((288, 192), np.float32)
    back = np.zeros((192, TOK), np.float32)
    rep = np.zeros((576, TOK), np.float32)
    fold = np.zeros((TOK, 576), np.float32)
    for r in range(WIN):
        for c in range(WIN):
            flipped = 143 - (c * WIN + r)
            p0[own_at(r, c), r * 16 + c] = 1
            p0[TOK + flipped, r * 16 + c] = 1
            back[r * 16 + c, own_at(r, c)] = 1
            for h in range(4):
                rep[c * 48 + h * WIN + r, flipped] = 1
                fold[own_at(r, c), c * 48 + h * WIN + r] = 1
    rep2 = np.zeros((576, TOK), np.float32)
    fold2 = np.zeros((2, 192, 288), np.float32)
    early = np.zeros((288, 304), np.float32)
    late = np.zeros((TOK, 160), np.float32)
    for b in range(2):
        for a in range(2):
            for c in range(HALF):
                for r in range(HALF):
                    at = r * HALF + c
                    for h in range(4):
                        row = a * TOK + c * 24 + h * HALF + r
                        rep2[b * 288 + row, b * 72 + a * 36 + at] = 1
                        fold2[b, (a * HALF + r) * 16 + b * HALF + c, row] = 1
                    for whole in (r, r + HALF):
                        key = (HALF - 1 - c) * WIN + WIN - 1 - whole
                        mine = (whole >= HALF) == (a == 0)
                        src = b * 72 + a * 36 + at if mine else 144 + 40 * (2 * a + b) + at
                        early[b * 144 + a * 72 + key, src] = 1
                        late[a * 72 + key, 40 * a + at if mine else 80 + 40 * a + at] = 1
    pick = np.zeros((384, 384), np.float32)
    for v in range(23):
        for r in range(WIN):
            pick[r * 23 + v, v * WIN + r] = 1
    order1 = np.zeros((192, 192), np.float32)
    order2 = np.zeros((96, 96), np.float32)
    for h in range(HEADS):
        for r in range(WIN):
            order1[h * WIN + r, r * HEADS + h] = 1
        for r in range(HALF):
            order2[h * HALF + r, r * HEADS + h] = 1
    return {
        "p0": p0,
        "pick": pick,
        "order1": np.concatenate([order1, order1], axis=1),
        "rep": rep,
        "fold": fold,
        "back": back,
        "order2": np.concatenate([order2, order2], axis=1),
        "rep2": rep2,
        "early": early,
        "late": late,
        "fold2": fold2,
    }


CONSTS = constants()
CNAMES = list(CONSTS)


def dot(a, b):
    return jnp.dot(a, b, preferred_element_type=F32)


def dot_nt(a, b):
    return lax.dot_general(a, b, (((1,), (1,)), ((), ())), preferred_element_type=F32)


def norm(data, gain):
    mean = jnp.mean(data, axis=-1, keepdims=True)
    centred = data - mean
    var = jnp.mean(centred * centred, axis=-1, keepdims=True)
    return (centred * lax.rsqrt(var + 1e-05) * gain).astype(BF16)


def split(values):
    high = values.astype(BF16)
    return high, (values - high.astype(F32)).astype(BF16)


def head_mask(size, width):
    row = lax.broadcasted_iota(jnp.int32, (4 * size, width), 0)
    lane = lax.broadcasted_iota(jnp.int32, (4 * size, width), 1)
    head = (row >= size).astype(jnp.int32) + (row >= 2 * size).astype(jnp.int32) + (row >= 3 * size).astype(jnp.int32)
    return head == ((lane // 32) & 3)


def masked(values, size):
    rows, width = values.shape
    mask = head_mask(size, width)
    kept = jnp.where(mask[None], values.reshape(rows // (4 * size), 4 * size, width), 0.0)
    return kept.reshape(rows, width).astype(BF16)


def offsets_table(table, padded, pick, order, start, count):
    padded[...] = jnp.zeros_like(padded)
    padded[:, :529] = table
    flat = padded[...] * LOG2E
    moved = [pltpu.roll(flat, (640 - 23 * r) % 640, 1) if r else flat for r in range(start, start + count)]
    rows = jnp.concatenate([m[:, :384] for m in moved], axis=0)
    high, low = split(rows)
    parts = jnp.concatenate([dot(high, pick).astype(BF16), dot(low, pick).astype(BF16)], axis=0)
    return dot(order, parts)


def attend(windows, size):
    units = [(w, slice(128 * g, 128 * g + 128), g) for w in windows for g in range(4)]
    ones = jnp.ones((TOK, 128), BF16)
    scores = []
    for (qhi, qlo, khi, klo, _, bias), at, g in units:
        left = jnp.concatenate([qhi[:, at], qlo[:, at], qhi[:, at]], axis=1)
        right = jnp.concatenate([khi[:, at], khi[:, at], klo[:, at]], axis=1)
        scores.append(dot_nt(left, right) + bias(g))
    expo = [jnp.exp2(x - jnp.max(x, axis=-1, keepdims=True)).astype(BF16) for x in scores]
    both = [dot(e, jnp.concatenate([w[4][:, at], ones], axis=1)) for e, (w, at, _) in zip(expo, units)]
    parts = [masked(x[:, :128] / x[:, 128:], size) for x in both]
    return [jnp.concatenate(parts[4 * i : 4 * i + 4], axis=1) for i in range(len(windows))]


def kernel(
    nlat, nlon, tok_h, gain1_h, wqkv1_h, wproj1_h, bias1_h, gain2_h, wqkv2_h, wproj2_h, bias2_h, *rest
):
    nc = len(CNAMES)
    const_h = dict(zip(CNAMES, rest[:nc]))
    out_h = rest[nc]
    (tok, gain1, wqkv1, wproj1, tab1, gain2, wqkv2, wproj2, tab2, tabn), rest = rest[nc + 1 : nc + 11], rest[nc + 11 :]
    const = dict(zip(CNAMES, rest[:nc]))
    (
        xpad, tpad, bias1, bias2, near, halo_lon, halo_lat, corner, own, pack, packed, unpack, keyval, ahi, alo,
        in_sem, out_sem, lon_send, lon_recv, lat_send, lat_recv, cor_send, cor_recv, tab_send, tab_recv,
    ) = rest[nc:]

    lat = lax.axis_index("lat")
    lon = lax.axis_index("lon")
    north = lax.rem(lat + nlat - 1, nlat)
    south = lax.rem(lat + 1, nlat)
    west = lax.rem(lon + nlon - 1, nlon)
    east = lax.rem(lon + 1, nlon)
    has_n = lat > 0
    has_s = lat < nlat - 1

    barrier = pltpu.get_barrier_semaphore()
    for peer in ((lat, west), (lat, east), (north, lon), (south, lon)):
        pl.semaphore_signal(barrier, inc=1, device_id=peer, device_id_type=MESH)

    loads = {}
    early_loads = [
        ("tab1", bias1_h, tab1), ("pick", const_h["pick"], const["pick"]), ("order1", const_h["order1"], const["order1"]),
        ("tok", tok_h, tok), ("p0", const_h["p0"], const["p0"]), ("gain1", gain1_h, gain1),
        ("wqkv1", wqkv1_h, wqkv1), ("rep", const_h["rep"], const["rep"]), ("fold", const_h["fold"], const["fold"]),
        ("wproj1", wproj1_h, wproj1), ("gain2", gain2_h, gain2), ("tab2", bias2_h, tab2),
    ]
    late_loads = [
        ("order2", const_h["order2"], const["order2"]), ("wqkv2", wqkv2_h, wqkv2), ("rep2", const_h["rep2"], const["rep2"]),
        ("back", const_h["back"], const["back"]), ("early", const_h["early"], const["early"]),
        ("late", const_h["late"], const["late"]), ("fold2", const_h["fold2"], const["fold2"]), ("wproj2", wproj2_h, wproj2),
    ]
    for i, (name, src, dst) in enumerate(early_loads + late_loads):
        loads[name] = pltpu.make_async_copy(src, dst, in_sem.at[i])
    for name, _, _ in early_loads:
        loads[name].start()

    def get(name):
        loads[name].wait()

    get("tab1")
    get("pick")
    get("order1")
    table = offsets_table(tab1[0], tpad, const["pick"][...], const["order1"][...], 0, WIN)
    for c in range(WIN):
        moved = table[:, WIN * c : WIN * c + TOK]
        for g in range(4):
            bias1[g, 48 * c : 48 * c + 48, :] = moved[48 * g : 48 * g + 48]

    get("tok")
    get("p0")
    xpad[...] = jnp.zeros_like(xpad)
    for r in range(WIN):
        xpad[16 * r : 16 * r + WIN, :] = tok[0, r]
    both = dot(const["p0"][...], xpad[...])
    mine = both[:TOK]
    get("gain1")
    normed = norm(both[TOK:], gain1[...])
    get("wqkv1")
    scale = LOG2E / math.sqrt(32.0)
    flat = dot(normed, wqkv1[...])
    qhi, qlo = split(flat[:, :DIM] * scale)
    khi, klo = split(flat[:, DIM : 2 * DIM])
    val = flat[:, 2 * DIM :].astype(BF16)
    get("rep")
    for name, _, _ in late_loads:
        loads[name].start()
    rep = const["rep"][...]
    (heads,) = attend(
        [(masked(dot(rep, qhi), WIN), masked(dot(rep, qlo), WIN), khi, klo, val, lambda g: bias1[g])], WIN
    )
    get("fold")
    get("wproj1")
    heads = dot(const["fold"][...], heads).astype(BF16)
    first = (mine + dot(heads, wproj1[...])).astype(BF16)
    get("gain2")
    normed = norm(first.astype(F32), gain2[...])
    own[...] = normed
    wide = normed.astype(F32)
    for a in range(2):
        for b in range(2):
            for j in range(4):
                at = 72 * b + 36 * a
                pack[a, b, 36 * j : 36 * j + 36, :] = wide[at : at + 36, 128 * j : 128 * j + 128]
    packed[...] = pack[...].astype(BF16)

    side_far = jnp.where(lax.rem(lon, nlon // 2) == 0, 0, 1)
    side_near = 1 - side_far
    border = jnp.logical_or(lax.rem(lon, nlon // 2) == 0, lax.rem(lon, nlon // 2) == nlon // 2 - 1)
    part0 = lax.rem(lat, 2)
    get("tab2")
    pl.semaphore_wait(barrier, 4)

    def remote(src, dst, send, recv, peer):
        return pltpu.make_async_remote_copy(
            src_ref=src, dst_ref=dst, send_sem=send, recv_sem=recv, device_id=peer, device_id_type=MESH
        )

    def edge(b, a):
        peer = jnp.where(b == 0, west, east)
        return remote(packed.at[a, b], halo_lon.at[1 - b, a], lon_send.at[b, a], lon_recv.at[1 - b, a], (lat, peer))

    send_tab = remote(tab2, tabn, tab_send, tab_recv, (south, lon))
    send_tab.start()
    edge(side_far, part0).start()
    to_n = remote(packed.at[0], halo_lat.at[1], lat_send.at[0], lat_recv.at[1], (north, lon))
    to_s = remote(packed.at[1], halo_lat.at[0], lat_send.at[1], lat_recv.at[0], (south, lon))

    for a, has in ((0, has_n), (1, has_s)):
        @pl.when(jnp.logical_not(has))
        def _(a=a):
            halo_lat[a] = jnp.zeros((2, TOK, 128), BF16)
            for b in range(2):
                corner[b, a] = jnp.zeros((TOK, 128), BF16)

    get("order2")

    def window_bias(a, ref):
        start = HALF if a == 0 else 0
        table = offsets_table(ref[0], tpad, const["pick"][...], const["order2"][...], start, HALF)
        cut = jnp.logical_not(has_n if a == 0 else has_s)
        lane = lax.rem(lax.broadcasted_iota(jnp.int32, (1, TOK), 1), WIN)
        other = (lane >= HALF) if a == 0 else (lane < HALF)
        shut = jnp.where(other, jnp.where(cut, -1e30, 0.0), 0.0)
        for c in range(WIN):
            moved = table[:, WIN * c : WIN * c + TOK] + shut
            b = 0 if c >= HALF else 1
            row = 24 * (c % HALF)
            for g in range(4):
                bias2[a, b, g, row : row + 24, :] = moved[24 * g : 24 * g + 24]

    def relay(b):
        for a in (part0, 1 - part0):
            remote(packed.at[a, b], halo_lon.at[b, a], lon_send.at[b, a], lon_recv.at[b, a], (lat, west)).wait_recv()
            peer = jnp.where(a == 0, north, south)

            @pl.when(jnp.where(a == 0, lat > 0, lat < nlat - 1))
            def _(a=a, peer=peer):
                remote(
                    halo_lon.at[b, a], corner.at[b, 1 - a], cor_send.at[b, a], cor_recv.at[b, 1 - a], (peer, lon)
                ).start()

    def settle(b):
        for a, has in ((0, has_n), (1, has_s)):
            @pl.when(has)
            def _(a=a):
                remote(
                    halo_lon.at[b, a], corner.at[b, a], cor_send.at[b, a], cor_recv.at[b, a], (north, lon)
                ).wait_recv()

    def tokens_of(quadrants):
        for i, ref in enumerate(quadrants):
            data = ref[...].astype(F32)
            for j in range(4):
                unpack[40 * i : 40 * i + 36, 128 * j : 128 * j + 128] = data[36 * j : 36 * j + 36]
        return unpack[...].astype(BF16)

    def side(b):
        new = tokens_of([halo_lon.at[b, 0], halo_lon.at[b, 1], corner.at[b, 0], corner.at[b, 1]])
        new = dot(dot(const["late"][...], new).astype(BF16), wqkv2[:, DIM:])
        for a in range(2):
            keyval[b, a, pl.ds(pl.multiple_of(72 * (1 - b), 8), 72), :] = new[72 * a : 72 * a + 72]
        windows = []
        for a in range(2):
            khi, klo = split(keyval[b, a, :, :DIM])
            val = keyval[b, a, :, DIM:].astype(BF16)
            at = pl.ds(TOK * a, TOK)
            windows.append((ahi[b, at], alo[b, at], khi, klo, val, lambda g, a=a: bias2[a, b, g]))
        return dot(const["fold2"][b], jnp.concatenate(attend(windows, HALF), axis=0))

    unpack[...] = jnp.zeros_like(unpack)
    window_bias(1, tab2)
    get("wqkv2")
    qhi, qlo = split(dot(normed, wqkv2[:, :DIM]) * scale)
    get("rep2")
    rep = const["rep2"][...]
    ahi[...] = masked(dot(rep, qhi), HALF).reshape(2, 288, DIM)
    alo[...] = masked(dot(rep, qlo), HALF).reshape(2, 288, DIM)
    edge(side_far, 1 - part0).start()
    for a in (part0, 1 - part0):
        edge(side_near, a).start()
    @pl.when(has_n)
    def _():
        to_n.start()

    @pl.when(has_s)
    def _():
        to_s.start()


    get("back")
    residual = dot(const["back"][...], first)
    get("early")
    get("late")
    get("fold2")
    get("wproj2")

    relay(side_near)

    @pl.when(jnp.logical_not(border))
    def _():
        relay(side_far)

    remote(tab2, tabn, tab_send, tab_recv, (south, lon)).wait_recv()
    window_bias(0, tabn)
    for a, has in ((0, has_n), (1, has_s)):
        @pl.when(has)
        def _(a=a):
            remote(packed.at[a], halo_lat.at[a], lat_send.at[a], lat_recv.at[a], (north, lon)).wait_recv()

    known = jnp.concatenate(
        [own[...], tokens_of([halo_lat.at[0, 0], halo_lat.at[0, 1], halo_lat.at[1, 0], halo_lat.at[1, 1]])], axis=0
    )
    known = dot(dot(const["early"][...], known).astype(BF16), wqkv2[:, DIM:])
    for b in range(2):
        for a in range(2):
            at = 144 * b + 72 * a
            keyval[b, a, 72 * b : 72 * b + 72, :] = known[at : at + 72]

    settle(side_near)
    near[...] = side(side_near)

    @pl.when(border)
    def _():
        relay(side_far)

    settle(side_far)
    heads = (near[...] + side(side_far)).astype(BF16)
    mixed = (residual + dot(heads, wproj2[...])).astype(BF16)
    for r in range(WIN):
        tok[0, r] = mixed[16 * r : 16 * r + WIN]
    store = pltpu.make_async_copy(tok, out_h, out_sem)
    store.start()

    for b in range(2):
        for a in range(2):
            edge(b, a).wait_send()
    send_tab.wait_send()
    for a, has, copy, peer in ((0, has_n, to_n, north), (1, has_s, to_s, south)):
        @pl.when(has)
        def _(a=a, copy=copy, peer=peer):
            copy.wait_send()
            for b in range(2):
                remote(
                    halo_lon.at[b, a], corner.at[b, 1 - a], cor_send.at[b, a], cor_recv.at[b, 1 - a], (peer, lon)
                ).wait_send()

    store.wait()


def shards(tokens, gain1, wqkv1, wproj1, bias1, gain2, wqkv2, wproj2, bias2):
    nlat = lax.axis_size("lat")
    nlon = lax.axis_size("lon")
    consts = [jnp.asarray(CONSTS[name], BF16) for name in CNAMES]
    dma = pltpu.SemaphoreType.DMA
    vmem = pltpu.VMEM
    args = [tokens, gain1.reshape(1, DIM), wqkv1, wproj1, bias1, gain2.reshape(1, DIM), wqkv2, wproj2, bias2]
    scratch = [vmem(x.shape, x.dtype) for x in args] + [vmem(bias2.shape, F32)]
    scratch += [vmem(x.shape, BF16) for x in consts]
    scratch += [
        vmem((192, DIM), BF16),
        vmem((HEADS, 640), F32),
        vmem((4, 576, TOK), F32),
        vmem((2, 2, 4, TOK, TOK), F32),
        vmem((192, DIM), F32),
        vmem((2, 2, TOK, 128), BF16),
        vmem((2, 2, TOK, 128), BF16),
        vmem((2, 2, TOK, 128), BF16),
        vmem((TOK, DIM), BF16),
        vmem((2, 2, TOK, 128), F32),
        vmem((2, 2, TOK, 128), BF16),
        vmem((160, DIM), F32),
        vmem((2, 2, TOK, 2 * DIM), F32),
        vmem((2, 288, DIM), BF16),
        vmem((2, 288, DIM), BF16),
        dma((len(args) + len(consts),)),
        dma(()),
        dma((2, 2)), dma((2, 2)),
        dma((2,)), dma((2,)),
        dma((2, 2)), dma((2, 2)),
        dma(()), dma(()),
    ]
    anywhere = pl.BlockSpec(memory_space=pl.ANY)
    return pl.pallas_call(
        functools.partial(kernel, nlat, nlon),
        out_shape=jax.ShapeDtypeStruct(tokens.shape, BF16),
        in_specs=[anywhere] * (len(args) + len(consts)),
        out_specs=anywhere,
        scratch_shapes=scratch,
        compiler_params=pltpu.CompilerParams(
            collective_id=0, has_side_effects=True, vmem_limit_bytes=62 * 1024 * 1024
        ),
        cost_estimate=pl.CostEstimate(flops=2_000_000_000, bytes_accessed=8_000_000, transcendentals=700_000),
        name="pair",
    )(*args, *consts)


def solution(mesh):
    placed = (
        P(None, "lat", "lon", None), P(), P(), P(), P("lat", None, None), P(), P(), P(), P("lat", None, None),
    )
    return jax.shard_map(
        shards, mesh=mesh, in_specs=placed, out_specs=P(None, "lat", "lon", None), check_vma=False
    )
```
